32 devices in a mesh: section: 4 (over y, x), seq: 4 (over z), head: 2 (over core).
Axes of the slice: x: 2, y: 2, z: 4, core: 2. Of those that a mesh axis runs over, the one named last changes fastest.
Arguments:
- queries: bfloat16 [4096, 4096], P(('section', 'seq'), 'head'), may hold values from -180 to 180
- keys: bfloat16 [4096, 1024], P(('section', 'seq'), 'head'), may hold values from -6 to 6
- values: bfloat16 [4096, 1024], P(('section', 'seq'), 'head'), may hold values from -6 to 6
- query_pooling_weight: float32 [4, 4096], P(None, 'head'), may hold values from -3 to 3
- key_pooling_weight: float32 [4, 1024], P(None, 'head'), may hold values from -3 to 3
- value_pooling_weight: float32 [4, 1024], P(None, 'head'), may hold values from -3 to 3
- up_weight: float32 [4, 4096], P(None, 'head'), may hold values from -8 to 8
- out_gain: float32 [4096], P('head'), may hold values from 0.1 to 1.9
Outputs:
- attended: bfloat16 [4096, 4096], P(('section', 'seq'), 'head')
The draws below stay inside these ranges and needn't reach their ends.
All inputs are finite; a program needn't handle non-finite values.
Results may differ from the reference program's by a relative error of at most 0.0067.
Values may be sent and summed in bfloat16 or wider, within the bound.
No kernel may reach another device: no remote copies, remote signals or barrier semaphores. Data moves between devices by JAX's collectives and lax.ppermute only.
A program may use at most 128 MiB of HBM per device.

```python
import jax
import jax.numpy as jnp
from jax import lax

QUERY_HEADS = 32
KEY_VALUE_HEADS = 8
HEAD_SIZE = 128
POOL_FACTOR = 4
WINDOW_LENGTH = 512
SEQUENCE_LENGTH = 4096
COARSE_LENGTH = 1024


def draw_pair(key):
    base_seed = jax.random.fold_in(key, 4242)
    random_seeds = jax.random.split(base_seed, 2)
    key_matrix = jnp.clip(jax.random.normal(random_seeds[0], (SEQUENCE_LENGTH, KEY_VALUE_HEADS * HEAD_SIZE), jnp.float32), -6.0, 6.0)
    query_array = jnp.clip(jax.random.normal(random_seeds[1], (SEQUENCE_LENGTH, QUERY_HEADS * HEAD_SIZE), jnp.float32), -6.0, 6.0)
    return (query_array, key_matrix)


def draw_queries(key, part):
    return draw_pair(key)[0].astype(jnp.bfloat16)


def draw_keys(key, part):
    return draw_pair(key)[1].astype(jnp.bfloat16)


def steps_of(own_key, dims, cuts, smallest, top_value):
    def one(dim, shards_of):
        draws = jax.random.uniform(jax.random.fold_in(jax.random.fold_in(own_key, 6), dim), (shards_of,), jnp.float32, smallest / len(cuts), top_value / len(cuts))
        return jnp.repeat(jnp.exp(draws), dims[dim] // shards_of).reshape((-1,) + (1,) * (len(dims) - dim - 1))

    level = one(*cuts[0])
    for cut in cuts[1:]:
        level = level * one(*cut)
    return level


def noise(rng, dims, scale, limit, cuts=(), kind=jnp.bfloat16):
    level = steps_of(rng, dims, cuts, -0.22, 0.18) if cuts else 1.0
    entries = jax.random.normal(rng, dims, jnp.float32) * scale * level
    return jnp.minimum(jnp.maximum(entries, -limit), limit).astype(kind)


def setup_inputs(seed: int = 0) -> dict:
    arg_keys = jax.random.split(jax.random.key(seed), 9)
    queries = draw_queries(jax.random.fold_in(arg_keys[8], 71), 0)
    keys = draw_keys(jax.random.fold_in(arg_keys[8], 71), 0)
    values = noise(arg_keys[2], (SEQUENCE_LENGTH, KEY_VALUE_HEADS * HEAD_SIZE), 1.0, 6.0, ((0, 16), (1, 2)))
    query_pooling_weight = noise(arg_keys[3], (POOL_FACTOR, QUERY_HEADS * HEAD_SIZE), POOL_FACTOR ** -0.5, 3.0, ((1, 2),), jnp.float32)
    key_pooling_weight = noise(arg_keys[4], (POOL_FACTOR, KEY_VALUE_HEADS * HEAD_SIZE), POOL_FACTOR ** -0.5, 3.0, ((1, 2),), jnp.float32)
    value_pooling_weight = noise(arg_keys[5], (POOL_FACTOR, KEY_VALUE_HEADS * HEAD_SIZE), POOL_FACTOR ** -0.5, 3.0, ((1, 2),), jnp.float32)
    up_weight = noise(arg_keys[6], (POOL_FACTOR, QUERY_HEADS * HEAD_SIZE), 2.0, 8.0, ((1, 2),), jnp.float32)
    out_gain = jnp.clip(1.0 + 0.18 * jax.random.normal(arg_keys[7], (QUERY_HEADS * HEAD_SIZE,), jnp.float32), 0.1, 1.9)
    return {"queries": queries, "keys": keys, "values": values, "query_pooling_weight": query_pooling_weight, "key_pooling_weight": key_pooling_weight, "value_pooling_weight": value_pooling_weight, "up_weight": up_weight, "out_gain": out_gain}


def pooled_tokens(source, weights):
    grouped = source.astype(jnp.float32).reshape(source.shape[0] // POOL_FACTOR, POOL_FACTOR, source.shape[1])
    return lax.optimization_barrier(lax.optimization_barrier(jnp.sum(grouped * weights[None], axis=1)).astype(jnp.bfloat16))

def attend_head(head_q, head_k, head_v, query_pos, key_pos, allowed_fn):
    scores = jnp.einsum('gqd,kd->gqk', head_q, head_k) * HEAD_SIZE ** (-0.5)
    allowed = allowed_fn(query_pos, key_pos)
    scores = jnp.where(allowed[None], scores, -jnp.inf)
    highest = lax.optimization_barrier(jnp.max(scores, axis=-1, keepdims=True))
    weights = jnp.exp(scores - highest)
    normalizer = lax.optimization_barrier(jnp.sum(weights, axis=-1))
    rounded = lax.optimization_barrier(weights.astype(jnp.bfloat16)).astype(jnp.float32)
    blended = jnp.einsum('gqk,kd->gqd', rounded, head_v)
    return blended / normalizer[..., None]

def window_mask(query_pos, key_pos):
    return (key_pos[None, :] <= query_pos[:, None]) & (key_pos[None, :] > query_pos[:, None] - WINDOW_LENGTH) & (key_pos[None, :] >= 0)

def causal_mask(query_pos, key_pos):
    return key_pos[None, :] <= query_pos[:, None]

def reference(queries, keys, values, query_pooling_weight, key_pooling_weight, value_pooling_weight, up_weight, out_gain):
    group_length = QUERY_HEADS // KEY_VALUE_HEADS
    padded_keys = jnp.concatenate([jnp.zeros((WINDOW_LENGTH, KEY_VALUE_HEADS * HEAD_SIZE), jnp.float32), keys.astype(jnp.float32)], axis=0)
    padded_values = jnp.concatenate([jnp.zeros((WINDOW_LENGTH, KEY_VALUE_HEADS * HEAD_SIZE), jnp.float32), values.astype(jnp.float32)], axis=0)
    every_query = queries.astype(jnp.float32)

    def fine_block(block_index):
        starting_row = block_index.astype(jnp.int32) * WINDOW_LENGTH
        query_block = lax.dynamic_slice_in_dim(every_query, starting_row, WINDOW_LENGTH, 0).reshape(WINDOW_LENGTH, KEY_VALUE_HEADS, group_length, HEAD_SIZE)
        key_block = lax.dynamic_slice_in_dim(padded_keys, starting_row, 2 * WINDOW_LENGTH, 0).reshape(2 * WINDOW_LENGTH, KEY_VALUE_HEADS, HEAD_SIZE)
        value_block = lax.dynamic_slice_in_dim(padded_values, starting_row, 2 * WINDOW_LENGTH, 0).reshape(2 * WINDOW_LENGTH, KEY_VALUE_HEADS, HEAD_SIZE)
        query_pos = starting_row + jnp.arange(WINDOW_LENGTH, dtype=jnp.int32)
        key_pos = starting_row - WINDOW_LENGTH + jnp.arange(2 * WINDOW_LENGTH, dtype=jnp.int32)

        def one_head(operands):
            return attend_head(operands[0], operands[1], operands[2], query_pos, key_pos, window_mask)
        heads_out = lax.map(one_head, (jnp.transpose(query_block, (1, 2, 0, 3)), jnp.transpose(key_block, (1, 0, 2)), jnp.transpose(value_block, (1, 0, 2))))
        return jnp.transpose(heads_out, (2, 0, 1, 3)).reshape(WINDOW_LENGTH, QUERY_HEADS * HEAD_SIZE)
    fine_out = lax.map(fine_block, jnp.arange(SEQUENCE_LENGTH // WINDOW_LENGTH, dtype=jnp.int32)).reshape(SEQUENCE_LENGTH, QUERY_HEADS * HEAD_SIZE)
    pooled_query_rows = pooled_tokens(queries, query_pooling_weight).astype(jnp.float32).reshape(COARSE_LENGTH, KEY_VALUE_HEADS, group_length, HEAD_SIZE)
    pooled_key_rows = jnp.transpose(pooled_tokens(keys, key_pooling_weight).astype(jnp.float32).reshape(COARSE_LENGTH, KEY_VALUE_HEADS, HEAD_SIZE), (1, 0, 2))
    pooled_value_rows = jnp.transpose(pooled_tokens(values, value_pooling_weight).astype(jnp.float32).reshape(COARSE_LENGTH, KEY_VALUE_HEADS, HEAD_SIZE), (1, 0, 2))
    key_pos_all = jnp.arange(COARSE_LENGTH, dtype=jnp.int32)

    def coarse_block(block_index):
        starting_row = block_index.astype(jnp.int32) * WINDOW_LENGTH
        query_block = lax.dynamic_slice_in_dim(pooled_query_rows, starting_row, WINDOW_LENGTH, 0)
        query_pos = starting_row + jnp.arange(WINDOW_LENGTH, dtype=jnp.int32)

        def one_head(operands):
            return attend_head(operands[0], operands[1], operands[2], query_pos, key_pos_all, causal_mask)
        heads_out = lax.map(one_head, (jnp.transpose(query_block, (1, 2, 0, 3)), pooled_key_rows, pooled_value_rows))
        return jnp.transpose(heads_out, (2, 0, 1, 3)).reshape(WINDOW_LENGTH, QUERY_HEADS * HEAD_SIZE)
    coarse_out = lax.map(coarse_block, jnp.arange(COARSE_LENGTH // WINDOW_LENGTH, dtype=jnp.int32)).reshape(COARSE_LENGTH, QUERY_HEADS * HEAD_SIZE)
    shifted = jnp.concatenate([jnp.zeros((1, QUERY_HEADS * HEAD_SIZE), jnp.float32), coarse_out[:-1]], axis=0)
    upsampled = (shifted[:, None, :] * up_weight[None]).reshape(SEQUENCE_LENGTH, QUERY_HEADS * HEAD_SIZE)
    combined = fine_out + upsampled
    mean_square = lax.optimization_barrier(jnp.mean(combined * combined, axis=1, keepdims=True))
    return (combined * lax.rsqrt(mean_square + 1e-05) * out_gain[None]).astype(jnp.bfloat16)
```

```python
import functools
import math

import jax
import jax.numpy as jnp
from jax import lax
from jax.experimental import pallas as pl
from jax.experimental.pallas import tpu as pltpu
from jax.sharding import PartitionSpec as P

HEAD_SIZE = 128
POOL_FACTOR = 4
WINDOW_LENGTH = 512
KEY_CHUNK = 1024
MASKED = -1e30
EXP2_SCALE = HEAD_SIZE ** (-0.5) * math.log2(math.e)
NT = (((1,), (1,)), ((), ()))
NN = (((1,), (0,)), ((), ()))


def params(mib=48):
    return pltpu.CompilerParams(vmem_limit_bytes=mib * 1024 * 1024)


def cost(flops, nbytes, exps=0):
    return pl.CostEstimate(flops=int(flops), bytes_accessed=int(nbytes), transcendentals=int(exps))


def dot(a, b, dims):
    return lax.dot_general(a, b, dims, preferred_element_type=jnp.float32)


def passed_along(value, axis, steps):
    count = lax.axis_size(axis)
    return lax.ppermute(value, axis, [(source, source + steps) for source in range(count - steps)])


def selection(pooled, tokens, first):
    row = lax.broadcasted_iota(jnp.int32, (POOL_FACTOR * pooled, tokens), 0)
    column = lax.broadcasted_iota(jnp.int32, (POOL_FACTOR * pooled, tokens), 1)
    wanted = POOL_FACTOR * (row % pooled + first) + row // pooled
    return jnp.where(column == wanted, 1.0, 0.0).astype(jnp.bfloat16)


def weighted(picked, weights, pooled):
    total = picked[:pooled] * weights[0:1]
    for i in range(1, POOL_FACTOR):
        total = total + picked[i * pooled : (i + 1) * pooled] * weights[i : i + 1]
    return total


def pool_kv_kernel(k_ref, v_ref, kw_ref, vw_ref, out_ref):
    tokens = k_ref.shape[0]
    pooled = tokens // POOL_FACTOR
    pick = selection(pooled, tokens, 0)
    both = jnp.concatenate([k_ref[...], v_ref[...]], axis=1)
    weights = jnp.concatenate([kw_ref[...], vw_ref[...]], axis=1)
    result = weighted(dot(pick, both, NN), weights, pooled).astype(jnp.bfloat16)
    for z in range(out_ref.shape[1]):
        out_ref[0, z] = result


def pool_kv(keys, values, kw, vw, copies):
    tokens, columns = keys.shape
    heads = columns // HEAD_SIZE
    pooled = tokens // POOL_FACTOR
    kv_spec = pl.BlockSpec((tokens, HEAD_SIZE), lambda h: (0, h))
    w_spec = pl.BlockSpec((POOL_FACTOR, HEAD_SIZE), lambda h: (0, h))
    return pl.pallas_call(
        pool_kv_kernel,
        grid=(heads,),
        in_specs=[kv_spec, kv_spec, w_spec, w_spec],
        out_specs=pl.BlockSpec((1, copies, pooled, 2 * HEAD_SIZE), lambda h: (h, 0, 0, 0)),
        out_shape=jax.ShapeDtypeStruct((heads, copies, pooled, 2 * HEAD_SIZE), jnp.bfloat16),
        compiler_params=params(),
        cost_estimate=cost(4 * tokens * tokens * columns, 4 * tokens * columns + 2 * copies * tokens * columns),
    )(keys, values, kw, vw)


def pool_q_kernel(q_ref, tail_ref, w_ref, out_ref):
    tokens = q_ref.shape[0]
    pooled = tokens // POOL_FACTOR
    tail_rows = tail_ref.shape[0]
    picked = dot(selection(pooled, tokens, -1), q_ref[...], NN)
    picked = picked + dot(selection(pooled, tail_rows, tail_rows // POOL_FACTOR - 1), tail_ref[...], NN)
    out_ref[0] = weighted(picked, w_ref[...], pooled).astype(jnp.bfloat16)


def pool_q(queries, tail, qw, heads):
    tokens, columns = queries.shape
    pooled = tokens // POOL_FACTOR
    width = columns // heads
    return pl.pallas_call(
        pool_q_kernel,
        grid=(heads,),
        in_specs=[
            pl.BlockSpec((tokens, width), lambda h: (0, h)),
            pl.BlockSpec((tail.shape[0], width), lambda h: (0, h)),
            pl.BlockSpec((POOL_FACTOR, width), lambda h: (0, h)),
        ],
        out_specs=pl.BlockSpec((1, pooled, width), lambda h: (h, 0, 0)),
        out_shape=jax.ShapeDtypeStruct((heads, pooled, width), jnp.bfloat16),
        compiler_params=params(),
        cost_estimate=cost(2 * tokens * tokens * columns, 3 * tokens * columns),
    )(queries, tail, qw)


def with_ones(values):
    return jnp.concatenate([values, jnp.ones_like(values)], axis=1)


def coarse_kernel(seq_count, z_ref, q_ref, kv_ref, out_ref):
    sections, pooled, width = q_ref.shape
    group = width // HEAD_SIZE
    rows = group * pooled
    z = z_ref[0]
    for s in range(sections):
        q = q_ref[s]
        stacked = jnp.concatenate([q[:, g * HEAD_SIZE : (g + 1) * HEAD_SIZE] for g in range(group)], axis=0)
        reach = (s + 1) * seq_count * pooled
        row = lax.broadcasted_iota(jnp.int32, (rows, 1), 0) % pooled
        query_pos = (s * seq_count + z) * pooled + row - 1
        highest = total = None
        for start in range(0, reach, KEY_CHUNK):
            size = min(KEY_CHUNK, reach - start)
            blocks = slice(start // pooled, (start + size) // pooled)
            keys = kv_ref[blocks, :, :HEAD_SIZE].reshape(size, HEAD_SIZE)
            values = kv_ref[blocks, :, HEAD_SIZE:].reshape(size, HEAD_SIZE)
            scores = dot(stacked, keys, NT)
            key_pos = start + lax.broadcasted_iota(jnp.int32, (rows, size), 1)
            scores = jnp.where(key_pos <= query_pos, scores, MASKED)
            newest = jnp.max(scores, axis=1, keepdims=True)
            if highest is not None:
                newest = jnp.maximum(newest, highest)
            weights = jnp.exp2((scores - newest) * EXP2_SCALE).astype(jnp.bfloat16)
            part = dot(weights, with_ones(values), NN)
            total = part if total is None else total * jnp.exp2((highest - newest) * EXP2_SCALE) + part
            highest = newest
        result = total[:, :HEAD_SIZE] / total[:, HEAD_SIZE:]
        result = jnp.where(query_pos >= 0, result, 0.0).astype(jnp.bfloat16)
        for g in range(group):
            out_ref[s, :, g * HEAD_SIZE : (g + 1) * HEAD_SIZE] = result[g * pooled : (g + 1) * pooled]


def coarse_attention(z, queries, kv, seq_count):
    sections, pooled, width = queries.shape
    pairs = queries.size // HEAD_SIZE * kv.shape[0] * pooled
    return pl.pallas_call(
        functools.partial(coarse_kernel, seq_count),
        in_specs=[
            pl.BlockSpec(memory_space=pltpu.SMEM),
            pl.BlockSpec(memory_space=pltpu.VMEM),
            pl.BlockSpec(memory_space=pltpu.VMEM),
        ],
        out_specs=pl.BlockSpec(memory_space=pltpu.VMEM),
        out_shape=jax.ShapeDtypeStruct(queries.shape, jnp.bfloat16),
        compiler_params=params(),
        cost_estimate=cost(4 * pairs * HEAD_SIZE, 2 * (2 * queries.size + kv.size), pairs),
    )(z, queries, kv)


def fine_kernel(pos_ref, q_ref, k0_ref, k1_ref, k2_ref, v0_ref, v1_ref, v2_ref, coarse_ref, up_ref, comb_ref, sq_ref):
    tokens, width = q_ref.shape
    pooled = tokens // POOL_FACTOR
    head = pl.program_id(0)
    position = pos_ref[0]
    bias1 = jnp.where(position >= 1, 0.0, MASKED).astype(jnp.float32)
    bias2 = jnp.where(position >= 2, 0.0, MASKED).astype(jnp.float32)
    row = lax.broadcasted_iota(jnp.int32, (tokens, tokens), 0)
    column = lax.broadcasted_iota(jnp.int32, (tokens, tokens), 1)
    own = column <= row
    keys = [ref[...] for ref in (k0_ref, k1_ref, k2_ref)]
    values = [with_ones(ref[...]) for ref in (v0_ref, v1_ref, v2_ref)]
    token = lax.broadcasted_iota(jnp.int32, (tokens, pooled), 0)
    spread = jnp.where(token // POOL_FACTOR == lax.broadcasted_iota(jnp.int32, (tokens, pooled), 1), 1.0, 0.0)
    upsampled = dot(spread.astype(jnp.bfloat16), coarse_ref[0], NN)
    up = up_ref[...]
    up = jnp.concatenate([up, up], axis=0)
    upsampled = (upsampled.reshape(tokens // 8, 8, width) * up[None]).reshape(tokens, width)
    squares = jnp.zeros((tokens, HEAD_SIZE), jnp.float32)
    for g in range(width // HEAD_SIZE):
        columns = slice(g * HEAD_SIZE, (g + 1) * HEAD_SIZE)
        q = q_ref[:, columns]
        outer = jnp.where(own, dot(q, keys[0], NT), dot(q, keys[2], NT) + bias2)
        inner = dot(q, keys[1], NT) + bias1
        highest = jnp.max(jnp.maximum(outer, inner), axis=1, keepdims=True)
        outer = jnp.exp2((outer - highest) * EXP2_SCALE)
        inner = jnp.exp2((inner - highest) * EXP2_SCALE).astype(jnp.bfloat16)
        first = jnp.where(own, outer, 0.0).astype(jnp.bfloat16)
        last = jnp.where(own, 0.0, outer).astype(jnp.bfloat16)
        total = dot(first, values[0], NN) + dot(inner, values[1], NN) + dot(last, values[2], NN)
        combined = total[:, :HEAD_SIZE] / total[:, HEAD_SIZE:] + upsampled[:, columns]
        comb_ref[:, columns] = combined
        squares = squares + combined * combined

    @pl.when(head == 0)
    def _():
        sq_ref[...] = squares

    @pl.when(head > 0)
    def _():
        sq_ref[...] += squares

    @pl.when(head == pl.num_programs(0) - 1)
    def _():
        sq_ref[...] = jnp.broadcast_to(jnp.sum(sq_ref[...], axis=1, keepdims=True), sq_ref.shape)


def fine_attention(position, queries, keys, values, coarse, up_weight):
    tokens, columns = queries.shape
    heads = keys[0].shape[1] // HEAD_SIZE
    width = columns // heads
    pooled = tokens // POOL_FACTOR
    kv_spec = pl.BlockSpec((tokens, HEAD_SIZE), lambda h: (0, h))
    wide = pl.BlockSpec((tokens, width), lambda h: (0, h))
    pairs = tokens * tokens * 3 * columns // HEAD_SIZE
    return pl.pallas_call(
        fine_kernel,
        grid=(heads,),
        in_specs=[pl.BlockSpec(memory_space=pltpu.SMEM), wide]
        + [kv_spec] * 6
        + [pl.BlockSpec((1, pooled, width), lambda h: (h, 0, 0)), pl.BlockSpec((POOL_FACTOR, width), lambda h: (0, h))],
        out_specs=[wide, pl.BlockSpec((tokens, HEAD_SIZE), lambda h: (0, 0))],
        out_shape=[
            jax.ShapeDtypeStruct((tokens, columns), jnp.float32),
            jax.ShapeDtypeStruct((tokens, HEAD_SIZE), jnp.float32),
        ],
        compiler_params=params(),
        cost_estimate=cost(4 * pairs * HEAD_SIZE, 12 * tokens * columns, pairs),
    )(position, queries, *keys, *values, coarse, up_weight)


def norm_kernel(full, comb_ref, mine_ref, other_ref, gain_ref, out_ref):
    mean = (mine_ref[:, :1] + other_ref[:, :1]) / full
    out_ref[...] = (comb_ref[...] * lax.rsqrt(mean + 1e-05) * gain_ref[...]).astype(jnp.bfloat16)


def normalized(combined, mine, other, gain, full):
    tokens, columns = combined.shape
    parts = 4
    wide = pl.BlockSpec((tokens, columns // parts), lambda h: (0, h))
    narrow = pl.BlockSpec((tokens, HEAD_SIZE), lambda h: (0, 0))
    return pl.pallas_call(
        functools.partial(norm_kernel, full),
        grid=(parts,),
        in_specs=[wide, narrow, narrow, pl.BlockSpec((1, columns // parts), lambda h: (0, h))],
        out_specs=wide,
        out_shape=jax.ShapeDtypeStruct((tokens, columns), jnp.bfloat16),
        compiler_params=params(),
        cost_estimate=cost(3 * tokens * columns, 6 * tokens * columns),
    )(combined, mine, other, gain)


def per_device(queries, keys, values, qw, kw, vw, up_weight, out_gain):
    tokens, columns = queries.shape
    heads = keys.shape[1] // HEAD_SIZE
    seq_count = lax.axis_size("seq")
    section_count = lax.axis_size("section")
    head_count = lax.axis_size("head")
    if WINDOW_LENGTH != 2 * tokens or heads != section_count or head_count != 2:
        raise ValueError("unsupported sizes")
    line = ("section", "seq")
    z = lax.axis_index("seq")
    position = lax.axis_index("section") * seq_count + z

    tail = passed_along(queries[-16:], line, 1)
    k1 = passed_along(keys, line, 1)
    v1 = passed_along(values, line, 1)
    pooled_kv = pool_kv(keys, values, kw, vw, seq_count)
    pooled_kv = pooled_kv.reshape((-1,) + pooled_kv.shape[2:])
    moved_kv = lax.all_to_all(pooled_kv, line, split_axis=0, concat_axis=0, tiled=True)
    pooled_q = pool_q(queries, tail, qw, heads)
    moved_q = lax.all_to_all(pooled_q, "section", split_axis=0, concat_axis=0, tiled=True)
    k2 = passed_along(k1, line, 1)
    v2 = passed_along(v1, line, 1)
    coarse = coarse_attention(z[None], moved_q, moved_kv, seq_count)
    coarse = lax.all_to_all(coarse, "section", split_axis=0, concat_axis=0, tiled=True)
    combined, mine = fine_attention(position[None], queries, (keys, k1, k2), (values, v1, v2), coarse, up_weight)
    other = lax.ppermute(mine, "head", [(0, 1), (1, 0)])
    return normalized(combined, mine, other, out_gain[None], head_count * columns)


def solution(mesh):
    rows = P(("section", "seq"), "head")
    return jax.shard_map(
        per_device,
        mesh=mesh,
        in_specs=(rows, rows, rows, P(None, "head"), P(None, "head"), P(None, "head"), P(None, "head"), P("head")),
        out_specs=rows,
        check_vma=False,
    )
```

```python
import functools
import math

import jax
import jax.numpy as jnp
from jax import lax
from jax.experimental import pallas as pl
from jax.experimental.pallas import tpu as pltpu
from jax.sharding import PartitionSpec as P

HEAD_SIZE = 128
POOL_FACTOR = 4
WINDOW_LENGTH = 512
CARRY_ROWS = 16
MASKED = -1e30
EXP2_SCALE = HEAD_SIZE ** (-0.5) * math.log2(math.e)
NT = (((1,), (1,)), ((), ()))
NN = (((1,), (0,)), ((), ()))
ANY = pl.BlockSpec(memory_space=pl.ANY)
VMEM = pl.BlockSpec(memory_space=pltpu.VMEM)
SMEM = pl.BlockSpec(memory_space=pltpu.SMEM)


def params(mib=40):
    return pltpu.CompilerParams(vmem_limit_bytes=mib * 1024 * 1024)


def cost(flops, nbytes, exps=0):
    return pl.CostEstimate(flops=int(flops), bytes_accessed=int(nbytes), transcendentals=int(exps))


def dot(a, b, dims):
    return lax.dot_general(a, b, dims, preferred_element_type=jnp.float32)


def head_columns(h, width=HEAD_SIZE):
    return pl.ds(pl.multiple_of(h * width, width), width)


def in_ring(value, axis):
    count = lax.axis_size(axis)
    return lax.ppermute(value, axis, [(source, (source + 1) % count) for source in range(count)])


def exchanged(value, axis, offset):
    count = lax.axis_size(axis)
    return lax.ppermute(value, axis, [(source, source ^ offset) for source in range(count)])


def gathered(value, axis):
    held = {0: value}
    bit = lax.axis_size(axis) // 2
    while bit:
        held.update({offset ^ bit: exchanged(array, axis, bit) for offset, array in list(held.items())})
        bit //= 2
    return [held[offset] for offset in range(len(held))]


def pool_kernel(my_ref, q_hbm, k_hbm, v_hbm, qw_hbm, kw_hbm, vw_hbm, *rest):
    heads = len(rest) - 5
    outs, (q_buf, kv_buf, qw_buf, kvw_buf, sems) = rest[:heads], rest[heads:]
    tokens = q_hbm.shape[0]
    width = q_hbm.shape[1] // heads
    pooled = tokens // POOL_FACTOR
    my = my_ref[0]
    left, right = pl.ds(0, HEAD_SIZE), pl.ds(HEAD_SIZE, HEAD_SIZE)
    copies = []
    for m in range(heads):
        h = my ^ m
        wide, narrow = head_columns(h, width), head_columns(h)
        pairs = [
            (k_hbm.at[:, narrow], kv_buf.at[m, :, left]),
            (v_hbm.at[:, narrow], kv_buf.at[m, :, right]),
            (kw_hbm.at[:, narrow], kvw_buf.at[m, :, left]),
            (vw_hbm.at[:, narrow], kvw_buf.at[m, :, right]),
            (q_hbm.at[:, wide], q_buf.at[m]),
            (qw_hbm.at[:, wide], qw_buf.at[m]),
        ]
        copies.append([pltpu.make_async_copy(a, b, sems.at[m, i]) for i, (a, b) in enumerate(pairs)])
    for group in copies:
        for copy in group:
            copy.start()
    row = lax.broadcasted_iota(jnp.int32, (tokens, tokens), 0)
    column = lax.broadcasted_iota(jnp.int32, (tokens, tokens), 1)
    wanted = POOL_FACTOR * (row % pooled) + row // pooled
    pick = jnp.where(column == wanted, 1.0, 0.0).astype(jnp.bfloat16)

    def weighted(rows, weights):
        picked = dot(pick, rows, NN)
        total = picked[:pooled] * weights[0:1]
        for i in range(1, POOL_FACTOR):
            total = total + picked[i * pooled : (i + 1) * pooled] * weights[i : i + 1]
        return total.astype(jnp.bfloat16)

    for m in range(heads):
        for copy in copies[m]:
            copy.wait()
        outs[m][:, :width] = weighted(q_buf[m], qw_buf[m])
        outs[m][:, width:] = weighted(kv_buf[m], kvw_buf[m])


def pool(my, queries, keys, values, qw, kw, vw):
    tokens, columns = queries.shape
    heads = keys.shape[1] // HEAD_SIZE
    width = columns // heads
    span = 2 * HEAD_SIZE
    payload = jax.ShapeDtypeStruct((tokens // POOL_FACTOR, width + span), jnp.bfloat16)
    return pl.pallas_call(
        pool_kernel,
        in_specs=[SMEM] + [ANY] * 6,
        out_specs=[VMEM] * heads,
        out_shape=[payload] * heads,
        scratch_shapes=[
            pltpu.VMEM((heads, tokens, width), jnp.bfloat16),
            pltpu.VMEM((heads, tokens, span), jnp.bfloat16),
            pltpu.VMEM((heads, POOL_FACTOR, width), jnp.float32),
            pltpu.VMEM((heads, POOL_FACTOR, span), jnp.float32),
            pltpu.SemaphoreType.DMA((heads, 6)),
        ],
        compiler_params=params(),
        cost_estimate=cost(3 * tokens * tokens * columns, 4 * tokens * columns),
    )(my, queries, keys, values, qw, kw, vw)


def stack_kernel(my_ref, *refs):
    payloads, out_ref = refs[:-1], refs[-1]
    sections = len(payloads)
    pooled, span = payloads[0].shape[0], out_ref.shape[1]
    width = payloads[0].shape[1] - span
    my = my_ref[0]
    parts = width // span
    row = lax.broadcasted_iota(jnp.int32, (CARRY_ROWS, span), 0)
    carry = jnp.zeros((CARRY_ROWS, span), jnp.float32)
    for m in range(sections):
        s = my ^ m
        out_ref[pl.ds(pl.multiple_of(s * pooled, pooled), pooled), :] = payloads[m][:, width:]
        last = payloads[m][pooled - 16 :, :width].astype(jnp.float32)[15:]
        for i in range(parts):
            carry = jnp.where(row == parts * s + i, last[:, i * span : (i + 1) * span], carry)
    out_ref[sections * pooled :, :] = carry.astype(jnp.bfloat16)


def stack(my, payloads):
    sections = len(payloads)
    pooled, columns = payloads[0].shape
    span = 2 * HEAD_SIZE
    return pl.pallas_call(
        stack_kernel,
        in_specs=[SMEM] + [VMEM] * sections,
        out_specs=VMEM,
        out_shape=jax.ShapeDtypeStruct((sections * pooled + CARRY_ROWS, span), jnp.bfloat16),
        compiler_params=params(),
        cost_estimate=cost(sections * pooled * span, 4 * sections * pooled * span),
    )(my, *payloads)


def with_ones(values):
    return jnp.concatenate([values, jnp.ones_like(values)], axis=1)


def coarse_kernel(sections, seq_count, place_ref, *refs):
    payloads, blocks = refs[:sections], refs[sections : sections + seq_count]
    outs = refs[sections + seq_count : -4]
    q_buf, kv_buf, carry_buf, out_buf = refs[-4:]
    pooled = payloads[0].shape[0]
    span = kv_buf.shape[2]
    width = payloads[0].shape[1] - span
    group = width // HEAD_SIZE
    rows = group * pooled
    parts = width // span
    my, z = place_ref[0], place_ref[1]
    for m in range(sections):
        q_buf[my ^ m] = payloads[m][:, :width]
    for m in range(seq_count):
        carry_buf[z ^ m] = blocks[m][sections * pooled :, :]
        for s in range(sections):
            at = pl.ds(pl.multiple_of((z ^ m) * pooled, pooled), pooled)
            kv_buf[s, at, :] = blocks[m][s * pooled : (s + 1) * pooled, :]
    before = carry_buf[jnp.where(z == 0, seq_count - 1, z - 1)].astype(jnp.float32)
    chunk = seq_count * pooled
    row = lax.broadcasted_iota(jnp.int32, (rows, chunk), 0) % pooled
    column = lax.broadcasted_iota(jnp.int32, (rows, chunk), 1)
    allowed = column < z * pooled + row
    first = lax.broadcasted_iota(jnp.int32, (rows, HEAD_SIZE), 0) % pooled == 0
    for s in range(sections):
        q = q_buf[s].astype(jnp.float32)
        shifted = jnp.concatenate([q[-1:], q[:-1]], axis=0)
        here = before[parts * s : parts * (s + 1)]
        if s > 0:
            here = jnp.where(z == 0, before[parts * (s - 1) : parts * s], here)
        pieces = []
        for g in range(group):
            at = g * HEAD_SIZE
            piece = here[at // span : at // span + 1, at % span : at % span + HEAD_SIZE]
            pieces.append(jnp.where(first[:pooled], piece, shifted[:, at : at + HEAD_SIZE]))
        stacked = jnp.concatenate(pieces, axis=0).astype(jnp.bfloat16)
        scores = [dot(stacked, kv_buf[c, :, :HEAD_SIZE], NT) for c in range(s + 1)]
        scores[s] = jnp.where(allowed, scores[s], MASKED)
        highest = functools.reduce(jnp.maximum, scores)
        highest = jnp.max(highest, axis=1, keepdims=True)
        total = None
        for c in range(s + 1):
            weights = jnp.exp2((scores[c] - highest) * EXP2_SCALE).astype(jnp.bfloat16)
            part = dot(weights, with_ones(kv_buf[c, :, HEAD_SIZE:]), NN)
            total = part if total is None else total + part
        result = total[:, :HEAD_SIZE] / total[:, HEAD_SIZE:]
        if s == 0:
            result = jnp.where(first & (z == 0), 0.0, result)
        result = result.astype(jnp.bfloat16)
        for g in range(group):
            out_buf[s, :, g * HEAD_SIZE : (g + 1) * HEAD_SIZE] = result[g * pooled : (g + 1) * pooled]
    for m in range(sections):
        outs[m][...] = out_buf[my ^ m]


def coarse_attention(place, payloads, blocks):
    sections, seq_count = len(payloads), len(blocks)
    pooled, columns = payloads[0].shape
    span = 2 * HEAD_SIZE
    width = columns - span
    pairs = sections * pooled * width // HEAD_SIZE * sections * seq_count * pooled
    return pl.pallas_call(
        functools.partial(coarse_kernel, sections, seq_count),
        in_specs=[SMEM] + [VMEM] * (sections + seq_count),
        out_specs=[VMEM] * sections,
        out_shape=[jax.ShapeDtypeStruct((pooled, width), jnp.bfloat16)] * sections,
        scratch_shapes=[
            pltpu.VMEM((sections, pooled, width), jnp.bfloat16),
            pltpu.VMEM((sections, seq_count * pooled, span), jnp.bfloat16),
            pltpu.VMEM((seq_count, CARRY_ROWS, span), jnp.bfloat16),
            pltpu.VMEM((sections, pooled, width), jnp.bfloat16),
        ],
        compiler_params=params(),
        cost_estimate=cost(4 * pairs * HEAD_SIZE, 4 * sections * seq_count * pooled * span, pairs),
    )(place, *payloads, *blocks)


def fine_kernel(pos_ref, q_hbm, k0_hbm, k1_hbm, k2_hbm, v0_hbm, v1_hbm, acc_ref, last_ref, q_buf, kv_buf, sems):
    heads, tokens, width = q_buf.shape
    group = width // HEAD_SIZE
    sources = (k0_hbm, k1_hbm, v0_hbm, v1_hbm, k2_hbm)

    def copies(h):
        narrow = head_columns(h)
        found = [
            pltpu.make_async_copy(ref.at[:, narrow], kv_buf.at[i, h], sems.at[i, h]) for i, ref in enumerate(sources)
        ]
        found.append(pltpu.make_async_copy(q_hbm.at[:, head_columns(h, width)], q_buf.at[h], sems.at[len(sources), h]))
        return found

    for h in range(heads):
        for copy in copies(h):
            copy.start()
    position = pos_ref[0]
    bias1 = jnp.where(position >= 1, 0.0, MASKED).astype(jnp.float32)
    bias2 = jnp.where(position >= 2, 0.0, MASKED).astype(jnp.float32)
    row = lax.broadcasted_iota(jnp.int32, (tokens, tokens), 0)
    column = lax.broadcasted_iota(jnp.int32, (tokens, tokens), 1)
    own = column <= row
    ones = jnp.ones((tokens, HEAD_SIZE), jnp.bfloat16)

    def one_head(h, carried):
        for copy in copies(h):
            copy.wait()
        k0, k1, v0, v1, k2 = [kv_buf[i, h] for i in range(len(sources))]
        v0, v1 = with_ones(v0), with_ones(v1)
        for g in range(group):
            q = q_buf[h, :, g * HEAD_SIZE : (g + 1) * HEAD_SIZE]
            outer = jnp.where(own, dot(q, k0, NT), dot(q, k2, NT) + bias2)
            inner = dot(q, k1, NT) + bias1
            highest = jnp.max(jnp.maximum(outer, inner), axis=1, keepdims=True)
            outer = jnp.exp2((outer - highest) * EXP2_SCALE)
            inner = jnp.exp2((inner - highest) * EXP2_SCALE).astype(jnp.bfloat16)
            first = jnp.where(own, outer, 0.0).astype(jnp.bfloat16)
            last = jnp.where(own, 0.0, outer)
            total = dot(first, v0, NN) + dot(inner, v1, NN)
            scale = 1.0 / (total[:, HEAD_SIZE:] + dot(last.astype(jnp.bfloat16), ones, NN))
            acc_ref[:, head_columns(h * group + g)] = total[:, :HEAD_SIZE] * scale
            scaled = last * jnp.concatenate([scale] * (tokens // HEAD_SIZE), axis=1)
            last_ref[:, head_columns(h * group + g, tokens)] = scaled.astype(jnp.bfloat16)
        return carried

    lax.fori_loop(0, heads, one_head, 0)


def fine_attention(position, queries, keys, values):
    tokens, columns = queries.shape
    heads = keys[0].shape[1] // HEAD_SIZE
    width = columns // heads
    pairs = tokens * tokens * 3 * columns // HEAD_SIZE
    return pl.pallas_call(
        fine_kernel,
        in_specs=[SMEM] + [ANY] * 6,
        out_specs=[VMEM, VMEM],
        out_shape=[
            jax.ShapeDtypeStruct((tokens, columns), jnp.float32),
            jax.ShapeDtypeStruct((tokens, columns // HEAD_SIZE * tokens), jnp.bfloat16),
        ],
        scratch_shapes=[
            pltpu.VMEM((heads, tokens, width), jnp.bfloat16),
            pltpu.VMEM((5, heads, tokens, HEAD_SIZE), jnp.bfloat16),
            pltpu.SemaphoreType.DMA((6, heads)),
        ],
        compiler_params=params(),
        cost_estimate=cost(4 * pairs * HEAD_SIZE, 12 * tokens * columns, pairs),
    )(position, queries, *keys, *values)


def join_kernel(my_ref, acc_ref, last_ref, v2_hbm, up_ref, *refs):
    sections = len(refs) - 5
    coarse, (comb_ref, sq_ref, v2_buf, coarse_buf, sem) = refs[:sections], refs[sections:]
    copy = pltpu.make_async_copy(v2_hbm, v2_buf, sem)
    copy.start()
    tokens, columns = acc_ref.shape
    heads = v2_buf.shape[1] // HEAD_SIZE
    width = columns // heads
    pooled = tokens // POOL_FACTOR
    my = my_ref[0]
    for m in range(sections):
        coarse_buf[my ^ m] = coarse[m][...]
    token = lax.broadcasted_iota(jnp.int32, (tokens, pooled), 0)
    spread = jnp.where(token // POOL_FACTOR == lax.broadcasted_iota(jnp.int32, (tokens, pooled), 1), 1.0, 0.0)
    spread = spread.astype(jnp.bfloat16)
    copy.wait()

    def one_head(h, squares):
        wide = head_columns(h, width)
        upsampled = dot(spread, coarse_buf[h], NN)
        up = up_ref[:, wide]
        up = jnp.concatenate([up, up], axis=0)
        upsampled = (upsampled.reshape(tokens // 8, 8, width) * up[None]).reshape(tokens, width)
        values = v2_buf[:, head_columns(h)]
        for g in range(width // HEAD_SIZE):
            at = h * (width // HEAD_SIZE) + g
            part = dot(last_ref[:, head_columns(at, tokens)], values, NN)
            here = slice(g * HEAD_SIZE, (g + 1) * HEAD_SIZE)
            combined = acc_ref[:, head_columns(at)] + part + upsampled[:, here]
            comb_ref[:, head_columns(at)] = combined
            squares = squares + combined * combined
        return squares

    squares = lax.fori_loop(0, heads, one_head, jnp.zeros((tokens, HEAD_SIZE), jnp.float32))
    sq_ref[...] = jnp.broadcast_to(jnp.sum(squares, axis=1, keepdims=True), sq_ref.shape)


def join(my, acc, last, values, up_weight, coarse):
    tokens, columns = acc.shape
    pooled, width = coarse[0].shape
    return pl.pallas_call(
        join_kernel,
        in_specs=[SMEM, VMEM, VMEM, ANY, VMEM] + [VMEM] * len(coarse),
        out_specs=[VMEM, VMEM],
        out_shape=[
            jax.ShapeDtypeStruct((tokens, columns), jnp.float32),
            jax.ShapeDtypeStruct((tokens, HEAD_SIZE), jnp.float32),
        ],
        scratch_shapes=[
            pltpu.VMEM(values.shape, jnp.bfloat16),
            pltpu.VMEM((len(coarse), pooled, width), jnp.bfloat16),
            pltpu.SemaphoreType.DMA,
        ],
        compiler_params=params(),
        cost_estimate=cost(2 * tokens * tokens * columns, 12 * tokens * columns),
    )(my, acc, last, values, up_weight, *coarse)


def norm_kernel(full, comb_ref, mine_ref, other_ref, gain_ref, out_hbm, buf, sems):
    parts, rows, columns = buf.shape
    copies = []
    for i in range(parts):
        here = pl.ds(i * rows, rows)
        mean = (mine_ref[here, :1] + other_ref[here, :1]) / full
        buf[i] = (comb_ref[here, :] * lax.rsqrt(mean + 1e-05) * gain_ref[...]).astype(jnp.bfloat16)
        copies.append(pltpu.make_async_copy(buf.at[i], out_hbm.at[here, :], sems.at[i]))
        copies[-1].start()
    for copy in copies:
        copy.wait()


def normalized(combined, mine, other, gain, full):
    tokens, columns = combined.shape
    parts = 4
    return pl.pallas_call(
        functools.partial(norm_kernel, full),
        in_specs=[VMEM] * 4,
        out_specs=ANY,
        out_shape=jax.ShapeDtypeStruct((tokens, columns), jnp.bfloat16),
        scratch_shapes=[
            pltpu.VMEM((parts, tokens // parts, columns), jnp.bfloat16),
            pltpu.SemaphoreType.DMA((parts,)),
        ],
        compiler_params=params(),
        cost_estimate=cost(3 * tokens * columns, 6 * tokens * columns),
    )(combined, mine, other, gain)


def per_device(queries, keys, values, qw, kw, vw, up_weight, out_gain):
    tokens, columns = queries.shape
    heads = keys.shape[1] // HEAD_SIZE
    seq_count = lax.axis_size("seq")
    section_count = lax.axis_size("section")
    head_count = lax.axis_size("head")
    if WINDOW_LENGTH != 2 * tokens or heads != section_count or head_count != 2:
        raise ValueError("unsupported sizes")
    line = ("section", "seq")
    section = lax.axis_index("section")
    z = lax.axis_index("seq")
    position = section * seq_count + z
    my = section[None]
    others = range(1, section_count)

    k1 = in_ring(keys, line)
    v1 = in_ring(values, line)
    payloads = pool(my, queries, keys, values, qw, kw, vw)
    payloads = [payloads[0]] + [exchanged(payloads[m], "section", m) for m in others]
    blocks = gathered(stack(my, payloads), "seq")
    k2 = in_ring(k1, line)
    v2 = in_ring(v1, line)
    coarse = coarse_attention(jnp.stack([section, z]), payloads, blocks)
    coarse = [coarse[0]] + [exchanged(coarse[m], "section", m) for m in others]
    acc, last = fine_attention(position[None], queries, (keys, k1, k2), (values, v1))
    combined, mine = join(my, acc, last, v2, up_weight, coarse)
    other = exchanged(mine, "head", 1)
    return normalized(combined, mine, other, out_gain[None], head_count * columns)


def solution(mesh):
    rows = P(("section", "seq"), "head")
    return jax.shard_map(
        per_device,
        mesh=mesh,
        in_specs=(rows, rows, rows, P(None, "head"), P(None, "head"), P(None, "head"), P(None, "head"), P("head")),
        out_specs=rows,
        check_vma=False,
    )
```

```python
import functools
import math

import jax
import jax.numpy as jnp
from jax import lax
from jax.experimental import pallas as pl
from jax.experimental.pallas import tpu as pltpu
from jax.sharding import PartitionSpec as P

HEAD_SIZE = 128
POOL_FACTOR = 4
WINDOW_LENGTH = 512
CARRY_ROWS = 16
MASKED = -1e30
EXP2_SCALE = HEAD_SIZE ** (-0.5) * math.log2(math.e)
NT = (((1,), (1,)), ((), ()))
NN = (((1,), (0,)), ((), ()))
ANY = pl.BlockSpec(memory_space=pl.ANY)
VMEM = pl.BlockSpec(memory_space=pltpu.VMEM)
SMEM = pl.BlockSpec(memory_space=pltpu.SMEM)


def params(mib=40):
    return pltpu.CompilerParams(vmem_limit_bytes=mib * 1024 * 1024)


def cost(flops, nbytes, exps=0):
    return pl.CostEstimate(flops=int(flops), bytes_accessed=int(nbytes), transcendentals=int(exps))


def dot(a, b, dims):
    return lax.dot_general(a, b, dims, preferred_element_type=jnp.float32)


def in_hbm(*arrays):
    return [pltpu.with_memory_space_constraint(array, pltpu.HBM) for array in arrays]


def head_columns(h, width=HEAD_SIZE):
    return pl.ds(pl.multiple_of(h * width, width), width)


def in_ring(value, axis, name):
    count = lax.axis_size(axis)
    with jax.named_scope(name):
        return lax.ppermute(value, axis, [(source, (source + 1) % count) for source in range(count)])


def exchanged(value, axis, offset, name):
    count = lax.axis_size(axis)
    with jax.named_scope(f"{name}{offset}"):
        return lax.ppermute(value, axis, [(source, source ^ offset) for source in range(count)])


def pool_kernel(my_ref, q_hbm, k_hbm, v_hbm, qw_hbm, kw_hbm, vw_hbm, *rest):
    heads = len(rest) - 5
    outs, (q_buf, kv_buf, qw_buf, kvw_buf, sems) = rest[:heads], rest[heads:]
    tokens = q_hbm.shape[0]
    width = q_hbm.shape[1] // heads
    pooled = tokens // POOL_FACTOR
    my = my_ref[0]
    left, right = pl.ds(0, HEAD_SIZE), pl.ds(HEAD_SIZE, HEAD_SIZE)
    copies = []
    for m in range(heads):
        h = my ^ m
        wide, narrow = head_columns(h, width), head_columns(h)
        pairs = [
            (k_hbm.at[:, narrow], kv_buf.at[m, :, left]),
            (v_hbm.at[:, narrow], kv_buf.at[m, :, right]),
            (kw_hbm.at[:, narrow], kvw_buf.at[m, :, left]),
            (vw_hbm.at[:, narrow], kvw_buf.at[m, :, right]),
            (q_hbm.at[:, wide], q_buf.at[m]),
            (qw_hbm.at[:, wide], qw_buf.at[m]),
        ]
        copies.append([pltpu.make_async_copy(a, b, sems.at[m, i]) for i, (a, b) in enumerate(pairs)])
    for group in copies:
        for copy in group:
            copy.start()
    row = lax.broadcasted_iota(jnp.int32, (tokens, tokens), 0)
    column = lax.broadcasted_iota(jnp.int32, (tokens, tokens), 1)
    wanted = POOL_FACTOR * (row % pooled) + row // pooled
    pick = jnp.where(column == wanted, 1.0, 0.0).astype(jnp.bfloat16)

    def weighted(rows, weights):
        picked = dot(pick, rows, NN)
        total = picked[:pooled] * weights[0:1]
        for i in range(1, POOL_FACTOR):
            total = total + picked[i * pooled : (i + 1) * pooled] * weights[i : i + 1]
        return total.astype(jnp.bfloat16)

    for m in range(heads):
        for copy in copies[m]:
            copy.wait()
        outs[m][:, :width] = weighted(q_buf[m], qw_buf[m])
        outs[m][:, width:] = weighted(kv_buf[m], kvw_buf[m])


def pool(my, queries, keys, values, qw, kw, vw):
    tokens, columns = queries.shape
    heads = keys.shape[1] // HEAD_SIZE
    width = columns // heads
    span = 2 * HEAD_SIZE
    payload = jax.ShapeDtypeStruct((tokens // POOL_FACTOR, width + span), jnp.bfloat16)
    return pl.pallas_call(
        pool_kernel,
        in_specs=[SMEM] + [ANY] * 6,
        out_specs=[VMEM] * heads,
        out_shape=[payload] * heads,
        scratch_shapes=[
            pltpu.VMEM((heads, tokens, width), jnp.bfloat16),
            pltpu.VMEM((heads, tokens, span), jnp.bfloat16),
            pltpu.VMEM((heads, POOL_FACTOR, width), jnp.float32),
            pltpu.VMEM((heads, POOL_FACTOR, span), jnp.float32),
            pltpu.SemaphoreType.DMA((heads, 6)),
        ],
        compiler_params=params(),
        cost_estimate=cost(1000, 1000),
    )(my, *in_hbm(queries, keys, values, qw, kw, vw))


def stack_kernel(my_ref, *refs):
    payloads, out_ref = refs[:-1], refs[-1]
    sections = len(payloads)
    pooled, span = payloads[0].shape[0], out_ref.shape[1]
    width = payloads[0].shape[1] - span
    my = my_ref[0]
    parts = width // span
    row = lax.broadcasted_iota(jnp.int32, (CARRY_ROWS, span), 0)
    carry = jnp.zeros((CARRY_ROWS, span), jnp.float32)
    for m in range(sections):
        s = my ^ m
        out_ref[pl.ds(pl.multiple_of(s * pooled, pooled), pooled), :] = payloads[m][:, width:]
        last = payloads[m][pooled - 16 :, :width].astype(jnp.float32)[15:]
        for i in range(parts):
            carry = jnp.where(row == parts * s + i, last[:, i * span : (i + 1) * span], carry)
    out_ref[sections * pooled :, :] = carry.astype(jnp.bfloat16)


def stack(my, payloads):
    sections = len(payloads)
    pooled, columns = payloads[0].shape
    span = 2 * HEAD_SIZE
    return pl.pallas_call(
        stack_kernel,
        in_specs=[SMEM] + [VMEM] * sections,
        out_specs=VMEM,
        out_shape=jax.ShapeDtypeStruct((sections * pooled + CARRY_ROWS, span), jnp.bfloat16),
        compiler_params=params(),
        cost_estimate=cost(1000, 1000),
    )(my, *payloads)


def with_ones(values):
    return jnp.concatenate([values, jnp.ones_like(values)], axis=1)


def coarse_kernel(sections, seq_count, place_ref, *refs):
    payloads, blocks = refs[:sections], refs[sections : sections + seq_count]
    outs = refs[sections + seq_count : -4]
    q_buf, kv_buf, carry_buf, out_buf = refs[-4:]
    pooled = payloads[0].shape[0]
    span = kv_buf.shape[2]
    width = payloads[0].shape[1] - span
    group = width // HEAD_SIZE
    rows = group * pooled
    parts = width // span
    my, z = place_ref[0], place_ref[1]
    for m in range(sections):
        q_buf[my ^ m] = payloads[m][:, :width]
    for m in range(seq_count):
        carry_buf[z ^ m] = blocks[m][sections * pooled :, :]
        for s in range(sections):
            at = pl.ds(pl.multiple_of((z ^ m) * pooled, pooled), pooled)
            kv_buf[s, at, :] = blocks[m][s * pooled : (s + 1) * pooled, :]
    before = carry_buf[jnp.where(z == 0, seq_count - 1, z - 1)].astype(jnp.float32)
    chunk = seq_count * pooled
    row = lax.broadcasted_iota(jnp.int32, (rows, chunk), 0) % pooled
    column = lax.broadcasted_iota(jnp.int32, (rows, chunk), 1)
    allowed = column < z * pooled + row
    first = lax.broadcasted_iota(jnp.int32, (rows, HEAD_SIZE), 0) % pooled == 0
    for s in range(sections):
        q = q_buf[s].astype(jnp.float32)
        shifted = jnp.concatenate([q[-1:], q[:-1]], axis=0)
        here = before[parts * s : parts * (s + 1)]
        if s > 0:
            here = jnp.where(z == 0, before[parts * (s - 1) : parts * s], here)
        pieces = []
        for g in range(group):
            at = g * HEAD_SIZE
            piece = here[at // span : at // span + 1, at % span : at % span + HEAD_SIZE]
            pieces.append(jnp.where(first[:pooled], piece, shifted[:, at : at + HEAD_SIZE]))
        stacked = jnp.concatenate(pieces, axis=0).astype(jnp.bfloat16)
        scores = [dot(stacked, kv_buf[c, :, :HEAD_SIZE], NT) for c in range(s + 1)]
        scores[s] = jnp.where(allowed, scores[s], MASKED)
        highest = functools.reduce(jnp.maximum, scores)
        highest = jnp.max(highest, axis=1, keepdims=True)
        total = None
        for c in range(s + 1):
            weights = jnp.exp2((scores[c] - highest) * EXP2_SCALE).astype(jnp.bfloat16)
            part = dot(weights, with_ones(kv_buf[c, :, HEAD_SIZE:]), NN)
            total = part if total is None else total + part
        result = total[:, :HEAD_SIZE] / total[:, HEAD_SIZE:]
        if s == 0:
            result = jnp.where(first & (z == 0), 0.0, result)
        result = result.astype(jnp.bfloat16)
        for g in range(group):
            out_buf[s, :, g * HEAD_SIZE : (g + 1) * HEAD_SIZE] = result[g * pooled : (g + 1) * pooled]
    for m in range(sections):
        outs[m][...] = out_buf[my ^ m]


def coarse_attention(place, payloads, blocks):
    sections, seq_count = len(payloads), len(blocks)
    pooled, columns = payloads[0].shape
    span = 2 * HEAD_SIZE
    width = columns - span
    pairs = sections * pooled * width // HEAD_SIZE * sections * seq_count * pooled
    return pl.pallas_call(
        functools.partial(coarse_kernel, sections, seq_count),
        in_specs=[SMEM] + [VMEM] * (sections + seq_count),
        out_specs=[VMEM] * sections,
        out_shape=[jax.ShapeDtypeStruct((pooled, width), jnp.bfloat16)] * sections,
        scratch_shapes=[
            pltpu.VMEM((sections, pooled, width), jnp.bfloat16),
            pltpu.VMEM((sections, seq_count * pooled, span), jnp.bfloat16),
            pltpu.VMEM((seq_count, CARRY_ROWS, span), jnp.bfloat16),
            pltpu.VMEM((sections, pooled, width), jnp.bfloat16),
        ],
        compiler_params=params(),
        cost_estimate=cost(4 * pairs * HEAD_SIZE, 4 * sections * seq_count * pooled * span, pairs),
    )(place, *payloads, *blocks)


def near_kernel(pos_ref, q_hbm, k0_hbm, k1_hbm, v0_hbm, v1_hbm, acc_ref, sum_ref, max_ref, q_buf, kv_buf, sems):
    heads, tokens, width = q_buf.shape
    group = width // HEAD_SIZE
    sources = (k0_hbm, k1_hbm, v0_hbm, v1_hbm)

    def copies(h):
        narrow = head_columns(h)
        found = [
            pltpu.make_async_copy(ref.at[:, narrow], kv_buf.at[i, h], sems.at[i, h]) for i, ref in enumerate(sources)
        ]
        found.append(pltpu.make_async_copy(q_hbm.at[:, head_columns(h, width)], q_buf.at[h], sems.at[len(sources), h]))
        return found

    for h in range(heads):
        for copy in copies(h):
            copy.start()
    bias = jnp.where(pos_ref[0] >= 1, 0.0, MASKED).astype(jnp.float32)
    row = lax.broadcasted_iota(jnp.int32, (tokens, tokens), 0)
    column = lax.broadcasted_iota(jnp.int32, (tokens, tokens), 1)
    own = jnp.concatenate([column <= row] * group, axis=0)

    def one_head(h, carried):
        for copy in copies(h):
            copy.wait()
        k0, k1, v0, v1 = [kv_buf[i, h] for i in range(len(sources))]
        q = jnp.concatenate([q_buf[h, :, g * HEAD_SIZE : (g + 1) * HEAD_SIZE] for g in range(group)], axis=0)
        outer = jnp.where(own, dot(q, k0, NT), MASKED)
        inner = dot(q, k1, NT) + bias
        highest = jnp.max(jnp.maximum(outer, inner), axis=1, keepdims=True)
        outer = jnp.exp2((outer - highest) * EXP2_SCALE).astype(jnp.bfloat16)
        inner = jnp.exp2((inner - highest) * EXP2_SCALE).astype(jnp.bfloat16)
        total = dot(outer, with_ones(v0), NN) + dot(inner, with_ones(v1), NN)
        highest = jnp.broadcast_to(highest, (group * tokens, HEAD_SIZE))
        for g in range(group):
            here = slice(g * tokens, (g + 1) * tokens)
            at = head_columns(h * group + g)
            acc_ref[:, at] = total[here, :HEAD_SIZE]
            sum_ref[:, at] = total[here, HEAD_SIZE:]
            max_ref[:, at] = highest[here]
        return carried

    lax.fori_loop(0, heads, one_head, 0)


def near_attention(position, queries, keys, values):
    tokens, columns = queries.shape
    heads = keys[0].shape[1] // HEAD_SIZE
    width = columns // heads
    pairs = tokens * tokens * 2 * columns // HEAD_SIZE
    return pl.pallas_call(
        near_kernel,
        in_specs=[SMEM] + [ANY] * 5,
        out_specs=[VMEM] * 3,
        out_shape=[jax.ShapeDtypeStruct((tokens, columns), jnp.float32)] * 3,
        scratch_shapes=[
            pltpu.VMEM((heads, tokens, width), jnp.bfloat16),
            pltpu.VMEM((4, heads, tokens, HEAD_SIZE), jnp.bfloat16),
            pltpu.SemaphoreType.DMA((5, heads)),
        ],
        compiler_params=params(),
        cost_estimate=cost(4 * pairs * HEAD_SIZE, 8 * tokens * columns, pairs),
    )(position, *in_hbm(queries, keys[0]), keys[1], *in_hbm(values[0]), values[1])


def far_kernel(pos_ref, q_hbm, k2_hbm, acc_in, sum_in, max_in, acc_ref, last_ref, q_buf, k_buf, sems):
    heads, tokens, width = q_buf.shape
    group = width // HEAD_SIZE

    def copies(h):
        return [
            pltpu.make_async_copy(k2_hbm.at[:, head_columns(h)], k_buf.at[h], sems.at[0, h]),
            pltpu.make_async_copy(q_hbm.at[:, head_columns(h, width)], q_buf.at[h], sems.at[1, h]),
        ]

    for h in range(heads):
        for copy in copies(h):
            copy.start()
    row = lax.broadcasted_iota(jnp.int32, (tokens, tokens), 0)
    column = lax.broadcasted_iota(jnp.int32, (tokens, tokens), 1)
    seen = jnp.concatenate([(column > row) & (pos_ref[0] >= 2)] * group, axis=0)
    ones = jnp.ones((tokens, HEAD_SIZE), jnp.bfloat16)

    def one_head(h, carried):
        for copy in copies(h):
            copy.wait()
        ats = [head_columns(h * group + g) for g in range(group)]
        q = jnp.concatenate([q_buf[h, :, g * HEAD_SIZE : (g + 1) * HEAD_SIZE] for g in range(group)], axis=0)
        scores = jnp.where(seen, dot(q, k_buf[h], NT), MASKED)
        before = jnp.concatenate([max_in[:, at] for at in ats], axis=0)
        highest = jnp.maximum(before, jnp.max(scores, axis=1, keepdims=True))
        spread = jnp.concatenate([highest] * (tokens // HEAD_SIZE), axis=1)
        weights = jnp.exp2((scores - spread) * EXP2_SCALE).astype(jnp.bfloat16)
        decay = jnp.exp2((before - highest) * EXP2_SCALE)
        total = jnp.concatenate([sum_in[:, at] for at in ats], axis=0) * decay + dot(weights, ones, NN)
        scale = 1.0 / total
        decay = decay * scale
        weights = (weights * jnp.concatenate([scale] * (tokens // HEAD_SIZE), axis=1)).astype(jnp.bfloat16)
        for g in range(group):
            here = slice(g * tokens, (g + 1) * tokens)
            acc_ref[:, ats[g]] = acc_in[:, ats[g]] * decay[here]
            last_ref[:, head_columns(h * group + g, tokens)] = weights[here]
        return carried

    lax.fori_loop(0, heads, one_head, 0)


def far_attention(position, queries, keys, acc, total, highest):
    tokens, columns = queries.shape
    heads = keys.shape[1] // HEAD_SIZE
    width = columns // heads
    pairs = tokens * tokens * columns // HEAD_SIZE
    return pl.pallas_call(
        far_kernel,
        in_specs=[SMEM, ANY, ANY] + [VMEM] * 3,
        out_specs=[VMEM] * 2,
        out_shape=[
            jax.ShapeDtypeStruct((tokens, columns), jnp.float32),
            jax.ShapeDtypeStruct((tokens, columns // HEAD_SIZE * tokens), jnp.bfloat16),
        ],
        scratch_shapes=[
            pltpu.VMEM((heads, tokens, width), jnp.bfloat16),
            pltpu.VMEM((heads, tokens, HEAD_SIZE), jnp.bfloat16),
            pltpu.SemaphoreType.DMA((2, heads)),
        ],
        compiler_params=params(),
        cost_estimate=cost(4 * pairs * HEAD_SIZE, 12 * tokens * columns, pairs),
    )(position, *in_hbm(queries), keys, acc, total, highest)


def join_kernel(my_ref, acc_ref, last_ref, v2_hbm, up_hbm, *refs):
    sections = len(refs) - 6
    coarse, (comb_ref, sq_ref, v2_buf, up_ref, coarse_buf, sems) = refs[:sections], refs[sections:]
    copies = [
        pltpu.make_async_copy(v2_hbm, v2_buf, sems.at[0]),
        pltpu.make_async_copy(up_hbm, up_ref, sems.at[1]),
    ]
    for copy in copies:
        copy.start()
    tokens, columns = acc_ref.shape
    heads = v2_buf.shape[1] // HEAD_SIZE
    width = columns // heads
    pooled = tokens // POOL_FACTOR
    my = my_ref[0]
    for m in range(sections):
        coarse_buf[my ^ m] = coarse[m][...]
    token = lax.broadcasted_iota(jnp.int32, (tokens, pooled), 0)
    spread = jnp.where(token // POOL_FACTOR == lax.broadcasted_iota(jnp.int32, (tokens, pooled), 1), 1.0, 0.0)
    spread = spread.astype(jnp.bfloat16)
    for copy in copies:
        copy.wait()

    def one_head(h, squares):
        wide = head_columns(h, width)
        upsampled = dot(spread, coarse_buf[h], NN)
        up = up_ref[:, wide]
        up = jnp.concatenate([up, up], axis=0)
        upsampled = (upsampled.reshape(tokens // 8, 8, width) * up[None]).reshape(tokens, width)
        values = v2_buf[:, head_columns(h)]
        for g in range(width // HEAD_SIZE):
            at = h * (width // HEAD_SIZE) + g
            part = dot(last_ref[:, head_columns(at, tokens)], values, NN)
            here = slice(g * HEAD_SIZE, (g + 1) * HEAD_SIZE)
            combined = acc_ref[:, head_columns(at)] + part + upsampled[:, here]
            comb_ref[:, head_columns(at)] = combined
            squares = squares + combined * combined
        return squares

    squares = lax.fori_loop(0, heads, one_head, jnp.zeros((tokens, HEAD_SIZE), jnp.float32))
    sq_ref[...] = jnp.broadcast_to(jnp.sum(squares, axis=1, keepdims=True), sq_ref.shape)


def join(my, acc, last, values, up_weight, coarse):
    tokens, columns = acc.shape
    pooled, width = coarse[0].shape
    return pl.pallas_call(
        join_kernel,
        in_specs=[SMEM, VMEM, VMEM, ANY, ANY] + [VMEM] * len(coarse),
        out_specs=[VMEM, VMEM],
        out_shape=[
            jax.ShapeDtypeStruct((tokens, columns), jnp.float32),
            jax.ShapeDtypeStruct((tokens, HEAD_SIZE), jnp.float32),
        ],
        scratch_shapes=[
            pltpu.VMEM(values.shape, jnp.bfloat16),
            pltpu.VMEM(up_weight.shape, jnp.float32),
            pltpu.VMEM((len(coarse), pooled, width), jnp.bfloat16),
            pltpu.SemaphoreType.DMA((2,)),
        ],
        compiler_params=params(),
        cost_estimate=cost(2 * tokens * tokens * columns, 12 * tokens * columns),
    )(my, acc, last, values, *in_hbm(up_weight), *coarse)


def norm_kernel(full, comb_ref, mine_ref, other_ref, gain_ref, out_hbm, buf, sems):
    parts, rows, columns = buf.shape
    copies = []
    for i in range(parts):
        here = pl.ds(i * rows, rows)
        mean = (mine_ref[here, :1] + other_ref[here, :1]) / full
        buf[i] = (comb_ref[here, :] * lax.rsqrt(mean + 1e-05) * gain_ref[...]).astype(jnp.bfloat16)
        copies.append(pltpu.make_async_copy(buf.at[i], out_hbm.at[here, :], sems.at[i]))
        copies[-1].start()
    for copy in copies:
        copy.wait()


def normalized(combined, mine, other, gain, full):
    tokens, columns = combined.shape
    parts = 4
    return pl.pallas_call(
        functools.partial(norm_kernel, full),
        in_specs=[VMEM] * 4,
        out_specs=ANY,
        out_shape=jax.ShapeDtypeStruct((tokens, columns), jnp.bfloat16),
        scratch_shapes=[
            pltpu.VMEM((parts, tokens // parts, columns), jnp.bfloat16),
            pltpu.SemaphoreType.DMA((parts,)),
        ],
        compiler_params=params(),
        cost_estimate=cost(3 * tokens * columns, 6 * tokens * columns),
    )(combined, mine, other, gain)


def per_device(queries, keys, values, qw, kw, vw, up_weight, out_gain):
    tokens, columns = queries.shape
    heads = keys.shape[1] // HEAD_SIZE
    seq_count = lax.axis_size("seq")
    section_count = lax.axis_size("section")
    head_count = lax.axis_size("head")
    if WINDOW_LENGTH != 2 * tokens or heads != section_count or head_count != 2:
        raise ValueError("unsupported sizes")
    line = ("section", "seq")
    section = lax.axis_index("section")
    z = lax.axis_index("seq")
    position = section * seq_count + z
    my = section[None]
    others = range(1, section_count)

    k1 = in_ring(keys, line, "first_keys")
    payloads = list(pool(my, queries, keys, values, qw, kw, vw))
    for m in others:
        payloads[m] = exchanged(payloads[m], "section", m, "pooled_to_heads")
    *payloads, late_values = lax.optimization_barrier((*payloads, values))
    v1 = in_ring(late_values, line, "first_values")
    stacked = stack(my, payloads)
    far = exchanged(stacked, "seq", 2, "pooled_far")
    near = exchanged(stacked, "seq", 1, "pooled_near")
    acc, total, highest = near_attention(position[None], queries, (keys, k1), (values, v1))
    far, near, acc = lax.optimization_barrier((far, near, acc))
    farther = exchanged(far, "seq", 1, "pooled_farther")
    far, k1 = lax.optimization_barrier((far, k1))
    k2 = in_ring(k1, line, "second_keys")
    farther, v1 = lax.optimization_barrier((farther, v1))
    v2 = in_ring(v1, line, "second_values")
    blocks = [stacked, near, far, farther]
    coarse = list(coarse_attention(jnp.stack([section, z]), payloads, blocks))
    for m in others:
        coarse[m] = exchanged(coarse[m], "section", m, "coarse_back")
    acc, last = far_attention(position[None], queries, k2, acc, total, highest)
    combined, mine = join(my, acc, last, v2, up_weight, coarse)
    other = exchanged(mine, "head", 1, "squares")
    return normalized(combined, mine, other, out_gain[None], head_count * columns)


def solution(mesh):
    rows = P(("section", "seq"), "head")
    return jax.shard_map(
        per_device,
        mesh=mesh,
        in_specs=(rows, rows, rows, P(None, "head"), P(None, "head"), P(None, "head"), P(None, "head"), P("head")),
        out_specs=rows,
        check_vma=False,
    )
```

```python
import functools
import math

import jax
import jax.numpy as jnp
from jax import lax
from jax.experimental import pallas as pl
from jax.experimental.pallas import tpu as pltpu
from jax.sharding import PartitionSpec as P

HEAD_SIZE = 128
POOL_FACTOR = 4
WINDOW_LENGTH = 512
CARRY_ROWS = 16
MASKED = -1e30
EXP2_SCALE = HEAD_SIZE ** (-0.5) * math.log2(math.e)
NT = (((1,), (1,)), ((), ()))
NN = (((1,), (0,)), ((), ()))
ANY = pl.BlockSpec(memory_space=pl.ANY)
VMEM = pl.BlockSpec(memory_space=pltpu.VMEM)
SMEM = pl.BlockSpec(memory_space=pltpu.SMEM)


def params(mib=40):
    return pltpu.CompilerParams(vmem_limit_bytes=mib * 1024 * 1024)


def cost(flops, nbytes, exps=0):
    return pl.CostEstimate(flops=int(flops), bytes_accessed=int(nbytes), transcendentals=int(exps))


def dot(a, b, dims):
    return lax.dot_general(a, b, dims, preferred_element_type=jnp.float32)


def in_hbm(*arrays):
    return [pltpu.with_memory_space_constraint(array, pltpu.HBM) for array in arrays]


def head_columns(h, width=HEAD_SIZE):
    return pl.ds(pl.multiple_of(h * width, width), width)


def in_ring(value, axis, name):
    count = lax.axis_size(axis)
    with jax.named_scope(name):
        return lax.ppermute(value, axis, [(source, (source + 1) % count) for source in range(count)])


def exchanged(value, axis, offset, name):
    count = lax.axis_size(axis)
    with jax.named_scope(f"{name}{offset}"):
        return lax.ppermute(value, axis, [(source, source ^ offset) for source in range(count)])


def pool_kernel(my_ref, q_hbm, k_hbm, v_hbm, qw_hbm, kw_hbm, vw_hbm, *rest):
    heads = len(rest) - 7
    outs, (q_buf, k_buf, v_buf, qw_buf, kw_buf, vw_buf, sems) = rest[:heads], rest[heads:]
    tokens = q_hbm.shape[0]
    width = q_hbm.shape[1] // heads
    pooled = tokens // POOL_FACTOR
    my = my_ref[0]
    pairs = (
        (k_hbm, k_buf),
        (v_hbm, v_buf),
        (kw_hbm, kw_buf),
        (vw_hbm, vw_buf),
        (qw_hbm, qw_buf),
        (q_hbm, q_buf),
    )
    copies = [pltpu.make_async_copy(a, b, sems.at[i]) for i, (a, b) in enumerate(pairs)]
    for copy in copies:
        copy.start()
    row = lax.broadcasted_iota(jnp.int32, (tokens, tokens), 0)
    column = lax.broadcasted_iota(jnp.int32, (tokens, tokens), 1)
    wanted = POOL_FACTOR * (row % pooled) + row // pooled
    pick = jnp.where(column == wanted, 1.0, 0.0).astype(jnp.bfloat16)

    def weighted(rows, weights):
        picked = dot(pick, rows, NN)
        total = picked[:pooled] * weights[0:1]
        for i in range(1, POOL_FACTOR):
            total = total + picked[i * pooled : (i + 1) * pooled] * weights[i : i + 1]
        return total.astype(jnp.bfloat16)

    for copy in copies[:4]:
        copy.wait()
    for m in range(heads):
        narrow = head_columns(my ^ m)
        rows = jnp.concatenate([k_buf[:, narrow], v_buf[:, narrow]], axis=1)
        weights = jnp.concatenate([kw_buf[:, narrow], vw_buf[:, narrow]], axis=1)
        outs[m][:, width:] = weighted(rows, weights)
    for copy in copies[4:]:
        copy.wait()
    for m in range(heads):
        wide = head_columns(my ^ m, width)
        outs[m][:, :width] = weighted(q_buf[:, wide], qw_buf[:, wide])


def pool(my, queries, keys, values, qw, kw, vw):
    tokens, columns = queries.shape
    heads = keys.shape[1] // HEAD_SIZE
    width = columns // heads
    span = 2 * HEAD_SIZE
    payload = jax.ShapeDtypeStruct((tokens // POOL_FACTOR, width + span), jnp.bfloat16)
    return pl.pallas_call(
        pool_kernel,
        in_specs=[SMEM] + [ANY] * 6,
        out_specs=[VMEM] * heads,
        out_shape=[payload] * heads,
        scratch_shapes=[
            pltpu.VMEM(queries.shape, jnp.bfloat16),
            pltpu.VMEM(keys.shape, jnp.bfloat16),
            pltpu.VMEM(values.shape, jnp.bfloat16),
            pltpu.VMEM(qw.shape, jnp.float32),
            pltpu.VMEM(kw.shape, jnp.float32),
            pltpu.VMEM(vw.shape, jnp.float32),
            pltpu.SemaphoreType.DMA((6,)),
        ],
        compiler_params=params(),
        cost_estimate=cost(1000, 1000),
    )(my, *in_hbm(queries, keys, values, qw, kw, vw))


def stack_kernel(my_ref, *refs):
    payloads, out_ref = refs[:-1], refs[-1]
    sections = len(payloads)
    pooled, span = payloads[0].shape[0], out_ref.shape[1]
    width = payloads[0].shape[1] - span
    my = my_ref[0]
    parts = width // span
    row = lax.broadcasted_iota(jnp.int32, (CARRY_ROWS, span), 0)
    carry = jnp.zeros((CARRY_ROWS, span), jnp.float32)
    for m in range(sections):
        s = my ^ m
        out_ref[pl.ds(pl.multiple_of(s * pooled, pooled), pooled), :] = payloads[m][:, width:]
        last = payloads[m][pooled - 16 :, :width].astype(jnp.float32)[15:]
        for i in range(parts):
            carry = jnp.where(row == parts * s + i, last[:, i * span : (i + 1) * span], carry)
    out_ref[sections * pooled :, :] = carry.astype(jnp.bfloat16)


def stack(my, payloads):
    sections = len(payloads)
    pooled, columns = payloads[0].shape
    span = 2 * HEAD_SIZE
    return pl.pallas_call(
        stack_kernel,
        in_specs=[SMEM] + [VMEM] * sections,
        out_specs=VMEM,
        out_shape=jax.ShapeDtypeStruct((sections * pooled + CARRY_ROWS, span), jnp.bfloat16),
        compiler_params=params(),
        cost_estimate=cost(1000, 1000),
    )(my, *payloads)


def with_ones(values):
    return jnp.concatenate([values, jnp.ones_like(values)], axis=1)


def coarse_kernel(sections, seq_count, place_ref, *refs):
    payloads, blocks = refs[:sections], refs[sections : sections + seq_count]
    outs = refs[sections + seq_count : -4]
    q_buf, kv_buf, carry_buf, out_buf = refs[-4:]
    pooled = payloads[0].shape[0]
    span = kv_buf.shape[2]
    width = payloads[0].shape[1] - span
    group = width // HEAD_SIZE
    rows = group * pooled
    parts = width // span
    my, z = place_ref[0], place_ref[1]
    for m in range(sections):
        q_buf[my ^ m] = payloads[m][:, :width]
    for m in range(seq_count):
        carry_buf[z ^ m] = blocks[m][sections * pooled :, :]
        for s in range(sections):
            at = pl.ds(pl.multiple_of((z ^ m) * pooled, pooled), pooled)
            kv_buf[s, at, :] = blocks[m][s * pooled : (s + 1) * pooled, :]
    before = carry_buf[jnp.where(z == 0, seq_count - 1, z - 1)].astype(jnp.float32)
    chunk = seq_count * pooled
    row = lax.broadcasted_iota(jnp.int32, (rows, chunk), 0) % pooled
    column = lax.broadcasted_iota(jnp.int32, (rows, chunk), 1)
    allowed = column < z * pooled + row
    first = lax.broadcasted_iota(jnp.int32, (rows, HEAD_SIZE), 0) % pooled == 0
    for s in range(sections):
        q = q_buf[s].astype(jnp.float32)
        shifted = jnp.concatenate([q[-1:], q[:-1]], axis=0)
        here = before[parts * s : parts * (s + 1)]
        if s > 0:
            here = jnp.where(z == 0, before[parts * (s - 1) : parts * s], here)
        pieces = []
        for g in range(group):
            at = g * HEAD_SIZE
            piece = here[at // span : at // span + 1, at % span : at % span + HEAD_SIZE]
            pieces.append(jnp.where(first[:pooled], piece, shifted[:, at : at + HEAD_SIZE]))
        stacked = jnp.concatenate(pieces, axis=0).astype(jnp.bfloat16)
        scores = [dot(stacked, kv_buf[c, :, :HEAD_SIZE], NT) for c in range(s + 1)]
        scores[s] = jnp.where(allowed, scores[s], MASKED)
        highest = functools.reduce(jnp.maximum, scores)
        highest = jnp.max(highest, axis=1, keepdims=True)
        total = None
        for c in range(s + 1):
            weights = jnp.exp2((scores[c] - highest) * EXP2_SCALE).astype(jnp.bfloat16)
            part = dot(weights, with_ones(kv_buf[c, :, HEAD_SIZE:]), NN)
            total = part if total is None else total + part
        result = total[:, :HEAD_SIZE] / total[:, HEAD_SIZE:]
        if s == 0:
            result = jnp.where(first & (z == 0), 0.0, result)
        result = result.astype(jnp.bfloat16)
        for g in range(group):
            out_buf[s, :, g * HEAD_SIZE : (g + 1) * HEAD_SIZE] = result[g * pooled : (g + 1) * pooled]
    for m in range(sections):
        outs[m][...] = out_buf[my ^ m]


def coarse_attention(place, payloads, blocks):
    sections, seq_count = len(payloads), len(blocks)
    pooled, columns = payloads[0].shape
    span = 2 * HEAD_SIZE
    width = columns - span
    pairs = sections * pooled * width // HEAD_SIZE * sections * seq_count * pooled
    return pl.pallas_call(
        functools.partial(coarse_kernel, sections, seq_count),
        in_specs=[SMEM] + [VMEM] * (sections + seq_count),
        out_specs=[VMEM] * sections,
        out_shape=[jax.ShapeDtypeStruct((pooled, width), jnp.bfloat16)] * sections,
        scratch_shapes=[
            pltpu.VMEM((sections, pooled, width), jnp.bfloat16),
            pltpu.VMEM((sections, seq_count * pooled, span), jnp.bfloat16),
            pltpu.VMEM((seq_count, CARRY_ROWS, span), jnp.bfloat16),
            pltpu.VMEM((sections, pooled, width), jnp.bfloat16),
        ],
        compiler_params=params(),
        cost_estimate=cost(4 * pairs * HEAD_SIZE, 4 * sections * seq_count * pooled * span, pairs),
    )(place, *payloads, *blocks)


def near_kernel(pos_ref, q_hbm, k0_hbm, k1_hbm, v0_hbm, v1_hbm, acc_ref, sum_ref, max_ref, q_buf, kv_buf, sems):
    heads, tokens, width = q_buf.shape
    group = width // HEAD_SIZE
    sources = (k0_hbm, k1_hbm, v0_hbm, v1_hbm)
    whole = [pltpu.make_async_copy(ref, kv_buf.at[i], sems.at[i]) for i, ref in enumerate(sources)]

    def q_copy(h):
        return pltpu.make_async_copy(q_hbm.at[:, head_columns(h, width)], q_buf.at[h], sems.at[len(sources) + h])

    whole[0].start()
    whole[1].start()
    q_copy(0).start()
    whole[2].start()
    whole[3].start()
    for h in range(1, heads):
        q_copy(h).start()
    bias = jnp.where(pos_ref[0] >= 1, 0.0, MASKED).astype(jnp.float32)
    row = lax.broadcasted_iota(jnp.int32, (tokens, tokens), 0)
    column = lax.broadcasted_iota(jnp.int32, (tokens, tokens), 1)
    own = jnp.concatenate([column <= row] * group, axis=0)

    for copy in whole:
        copy.wait()

    def one_head(h, carried):
        q_copy(h).wait()
        k0, k1, v0, v1 = [kv_buf[i, :, head_columns(h)] for i in range(len(sources))]
        q = jnp.concatenate([q_buf[h, :, g * HEAD_SIZE : (g + 1) * HEAD_SIZE] for g in range(group)], axis=0)
        outer = jnp.where(own, dot(q, k0, NT), MASKED)
        inner = dot(q, k1, NT) + bias
        highest = jnp.max(jnp.maximum(outer, inner), axis=1, keepdims=True)
        outer = jnp.exp2((outer - highest) * EXP2_SCALE).astype(jnp.bfloat16)
        inner = jnp.exp2((inner - highest) * EXP2_SCALE).astype(jnp.bfloat16)
        total = dot(outer, with_ones(v0), NN) + dot(inner, with_ones(v1), NN)
        highest = jnp.broadcast_to(highest, (group * tokens, HEAD_SIZE))
        for g in range(group):
            here = slice(g * tokens, (g + 1) * tokens)
            at = head_columns(h * group + g)
            acc_ref[:, at] = total[here, :HEAD_SIZE]
            sum_ref[:, at] = total[here, HEAD_SIZE:]
            max_ref[:, at] = highest[here]
        return carried

    lax.fori_loop(0, heads, one_head, 0)


def near_attention(position, queries, keys, values):
    tokens, columns = queries.shape
    heads = keys[0].shape[1] // HEAD_SIZE
    width = columns // heads
    pairs = tokens * tokens * 2 * columns // HEAD_SIZE
    return pl.pallas_call(
        near_kernel,
        in_specs=[SMEM] + [ANY] * 5,
        out_specs=[VMEM] * 3,
        out_shape=[jax.ShapeDtypeStruct((tokens, columns), jnp.float32)] * 3,
        scratch_shapes=[
            pltpu.VMEM((heads, tokens, width), jnp.bfloat16),
            pltpu.VMEM((4,) + values[0].shape, jnp.bfloat16),
            pltpu.SemaphoreType.DMA((4 + heads,)),
        ],
        compiler_params=params(),
        cost_estimate=cost(4 * pairs * HEAD_SIZE, 8 * tokens * columns, pairs),
    )(position, *in_hbm(queries, keys[0]), keys[1], *in_hbm(values[0]), values[1])


def far_kernel(pos_ref, q_hbm, k2_hbm, acc_in, sum_in, max_in, acc_ref, last_ref, q_buf, k_buf, sems):
    heads, tokens, width = q_buf.shape
    group = width // HEAD_SIZE

    k_copy = pltpu.make_async_copy(k2_hbm, k_buf, sems.at[heads])

    def q_copy(h):
        return pltpu.make_async_copy(q_hbm.at[:, head_columns(h, width)], q_buf.at[h], sems.at[h])

    k_copy.start()
    for h in range(heads):
        q_copy(h).start()
    row = lax.broadcasted_iota(jnp.int32, (tokens, tokens), 0)
    column = lax.broadcasted_iota(jnp.int32, (tokens, tokens), 1)
    seen = jnp.concatenate([(column > row) & (pos_ref[0] >= 2)] * group, axis=0)
    ones = jnp.ones((tokens, HEAD_SIZE), jnp.bfloat16)

    k_copy.wait()

    def one_head(h, carried):
        q_copy(h).wait()
        ats = [head_columns(h * group + g) for g in range(group)]
        q = jnp.concatenate([q_buf[h, :, g * HEAD_SIZE : (g + 1) * HEAD_SIZE] for g in range(group)], axis=0)
        scores = jnp.where(seen, dot(q, k_buf[:, head_columns(h)], NT), MASKED)
        before = jnp.concatenate([max_in[:, at] for at in ats], axis=0)
        highest = jnp.maximum(before, jnp.max(scores, axis=1, keepdims=True))
        spread = jnp.concatenate([highest] * (tokens // HEAD_SIZE), axis=1)
        weights = jnp.exp2((scores - spread) * EXP2_SCALE).astype(jnp.bfloat16)
        decay = jnp.exp2((before - highest) * EXP2_SCALE)
        total = jnp.concatenate([sum_in[:, at] for at in ats], axis=0) * decay + dot(weights, ones, NN)
        scale = 1.0 / total
        decay = decay * scale
        weights = (weights * jnp.concatenate([scale] * (tokens // HEAD_SIZE), axis=1)).astype(jnp.bfloat16)
        for g in range(group):
            here = slice(g * tokens, (g + 1) * tokens)
            acc_ref[:, ats[g]] = acc_in[:, ats[g]] * decay[here]
            last_ref[:, head_columns(h * group + g, tokens)] = weights[here]
        return carried

    lax.fori_loop(0, heads, one_head, 0)


def far_attention(position, queries, keys, acc, total, highest):
    tokens, columns = queries.shape
    heads = keys.shape[1] // HEAD_SIZE
    width = columns // heads
    pairs = tokens * tokens * columns // HEAD_SIZE
    return pl.pallas_call(
        far_kernel,
        in_specs=[SMEM, ANY, ANY] + [VMEM] * 3,
        out_specs=[VMEM] * 2,
        out_shape=[
            jax.ShapeDtypeStruct((tokens, columns), jnp.float32),
            jax.ShapeDtypeStruct((tokens, columns // HEAD_SIZE * tokens), jnp.bfloat16),
        ],
        scratch_shapes=[
            pltpu.VMEM((heads, tokens, width), jnp.bfloat16),
            pltpu.VMEM(keys.shape, jnp.bfloat16),
            pltpu.SemaphoreType.DMA((heads + 1,)),
        ],
        compiler_params=params(),
        cost_estimate=cost(4 * pairs * HEAD_SIZE, 12 * tokens * columns, pairs),
    )(position, *in_hbm(queries), keys, acc, total, highest)


def join_kernel(my_ref, acc_ref, last_ref, v2_hbm, up_hbm, *refs):
    sections = len(refs) - 6
    coarse, (comb_ref, sq_ref, v2_buf, up_ref, coarse_buf, sems) = refs[:sections], refs[sections:]
    copies = [
        pltpu.make_async_copy(v2_hbm, v2_buf, sems.at[0]),
        pltpu.make_async_copy(up_hbm, up_ref, sems.at[1]),
    ]
    for copy in copies:
        copy.start()
    tokens, columns = acc_ref.shape
    heads = v2_buf.shape[1] // HEAD_SIZE
    width = columns // heads
    pooled = tokens // POOL_FACTOR
    my = my_ref[0]
    for m in range(sections):
        coarse_buf[my ^ m] = coarse[m][...]
    token = lax.broadcasted_iota(jnp.int32, (tokens, pooled), 0)
    spread = jnp.where(token // POOL_FACTOR == lax.broadcasted_iota(jnp.int32, (tokens, pooled), 1), 1.0, 0.0)
    spread = spread.astype(jnp.bfloat16)
    for copy in copies:
        copy.wait()

    def one_head(h, squares):
        wide = head_columns(h, width)
        upsampled = dot(spread, coarse_buf[h], NN)
        up = up_ref[:, wide]
        up = jnp.concatenate([up, up], axis=0)
        upsampled = (upsampled.reshape(tokens // 8, 8, width) * up[None]).reshape(tokens, width)
        values = v2_buf[:, head_columns(h)]
        for g in range(width // HEAD_SIZE):
            at = h * (width // HEAD_SIZE) + g
            part = dot(last_ref[:, head_columns(at, tokens)], values, NN)
            here = slice(g * HEAD_SIZE, (g + 1) * HEAD_SIZE)
            combined = acc_ref[:, head_columns(at)] + part + upsampled[:, here]
            comb_ref[:, head_columns(at)] = combined
            squares = squares + combined * combined
        return squares

    squares = lax.fori_loop(0, heads, one_head, jnp.zeros((tokens, HEAD_SIZE), jnp.float32))
    sq_ref[...] = jnp.broadcast_to(jnp.sum(squares, axis=1, keepdims=True), sq_ref.shape)


def join(my, acc, last, values, up_weight, coarse):
    tokens, columns = acc.shape
    pooled, width = coarse[0].shape
    return pl.pallas_call(
        join_kernel,
        in_specs=[SMEM, VMEM, VMEM, ANY, ANY] + [VMEM] * len(coarse),
        out_specs=[VMEM, VMEM],
        out_shape=[
            jax.ShapeDtypeStruct((tokens, columns), jnp.float32),
            jax.ShapeDtypeStruct((tokens, HEAD_SIZE), jnp.float32),
        ],
        scratch_shapes=[
            pltpu.VMEM(values.shape, jnp.bfloat16),
            pltpu.VMEM(up_weight.shape, jnp.float32),
            pltpu.VMEM((len(coarse), pooled, width), jnp.bfloat16),
            pltpu.SemaphoreType.DMA((2,)),
        ],
        compiler_params=params(),
        cost_estimate=cost(2 * tokens * tokens * columns, 12 * tokens * columns),
    )(my, acc, last, values, *in_hbm(up_weight), *coarse)


def norm_kernel(full, comb_ref, mine_ref, other_ref, gain_ref, out_hbm, buf, sems):
    parts, rows, columns = buf.shape
    copies = []
    for i in range(parts):
        here = pl.ds(i * rows, rows)
        mean = (mine_ref[here, :1] + other_ref[here, :1]) / full
        buf[i] = (comb_ref[here, :] * lax.rsqrt(mean + 1e-05) * gain_ref[...]).astype(jnp.bfloat16)
        copies.append(pltpu.make_async_copy(buf.at[i], out_hbm.at[here, :], sems.at[i]))
        copies[-1].start()
    for copy in copies:
        copy.wait()


def normalized(combined, mine, other, gain, full):
    tokens, columns = combined.shape
    parts = 4
    return pl.pallas_call(
        functools.partial(norm_kernel, full),
        in_specs=[VMEM] * 4,
        out_specs=ANY,
        out_shape=jax.ShapeDtypeStruct((tokens, columns), jnp.bfloat16),
        scratch_shapes=[
            pltpu.VMEM((parts, tokens // parts, columns), jnp.bfloat16),
            pltpu.SemaphoreType.DMA((parts,)),
        ],
        compiler_params=params(),
        cost_estimate=cost(3 * tokens * columns, 6 * tokens * columns),
    )(combined, mine, other, gain)


def per_device(queries, keys, values, qw, kw, vw, up_weight, out_gain):
    tokens, columns = queries.shape
    heads = keys.shape[1] // HEAD_SIZE
    seq_count = lax.axis_size("seq")
    section_count = lax.axis_size("section")
    head_count = lax.axis_size("head")
    if WINDOW_LENGTH != 2 * tokens or heads != section_count or head_count != 2:
        raise ValueError("unsupported sizes")
    line = ("section", "seq")
    section = lax.axis_index("section")
    z = lax.axis_index("seq")
    position = section * seq_count + z
    my = section[None]
    others = range(1, section_count)

    k1 = in_ring(keys, line, "first_keys")
    payloads = list(pool(my, queries, keys, values, qw, kw, vw))
    for m in others:
        payloads[m] = exchanged(payloads[m], "section", m, "pooled_to_heads")
    *payloads, late_values = lax.optimization_barrier((*payloads, values))
    v1 = in_ring(late_values, line, "first_values")
    stacked = stack(my, payloads)
    far = exchanged(stacked, "seq", 2, "pooled_far")
    near = exchanged(stacked, "seq", 1, "pooled_near")
    acc, total, highest = near_attention(position[None], queries, (keys, k1), (values, v1))
    far, near, acc = lax.optimization_barrier((far, near, acc))
    farther = exchanged(far, "seq", 1, "pooled_farther")
    far, k1 = lax.optimization_barrier((far, k1))
    k2 = in_ring(k1, line, "second_keys")
    farther, v1 = lax.optimization_barrier((farther, v1))
    v2 = in_ring(v1, line, "second_values")
    blocks = [stacked, near, far, farther]
    coarse = list(coarse_attention(jnp.stack([section, z]), payloads, blocks))
    for m in others:
        coarse[m] = exchanged(coarse[m], "section", m, "coarse_back")
    acc, last = far_attention(position[None], queries, k2, acc, total, highest)
    combined, mine = join(my, acc, last, v2, up_weight, coarse)
    other = exchanged(mine, "head", 1, "squares")
    return normalized(combined, mine, other, out_gain[None], head_count * columns)


def solution(mesh):
    rows = P(("section", "seq"), "head")
    return jax.shard_map(
        per_device,
        mesh=mesh,
        in_specs=(rows, rows, rows, P(None, "head"), P(None, "head"), P(None, "head"), P(None, "head"), P("head")),
        out_specs=rows,
        check_vma=False,
    )
```

```python
import functools
import math

import jax
import jax.numpy as jnp
from jax import lax
from jax.experimental import pallas as pl
from jax.experimental.pallas import tpu as pltpu
from jax.sharding import PartitionSpec as P

HEAD_SIZE = 128
POOL_FACTOR = 4
WINDOW_LENGTH = 512
CARRY_ROWS = 16
MASKED = -1e30
EXP2_SCALE = HEAD_SIZE ** (-0.5) * math.log2(math.e)
NT = (((1,), (1,)), ((), ()))
NN = (((1,), (0,)), ((), ()))
ANY = pl.BlockSpec(memory_space=pl.ANY)
VMEM = pl.BlockSpec(memory_space=pltpu.VMEM)
SMEM = pl.BlockSpec(memory_space=pltpu.SMEM)


def params(mib=40):
    return pltpu.CompilerParams(vmem_limit_bytes=mib * 1024 * 1024)


def cost(flops, nbytes, exps=0):
    return pl.CostEstimate(flops=int(flops), bytes_accessed=int(nbytes), transcendentals=int(exps))


def dot(a, b, dims):
    return lax.dot_general(a, b, dims, preferred_element_type=jnp.float32)


def in_hbm(*arrays):
    return [pltpu.with_memory_space_constraint(array, pltpu.HBM) for array in arrays]


def head_columns(h, width=HEAD_SIZE):
    if isinstance(h, int):
        return slice(h * width, (h + 1) * width)
    return pl.ds(pl.multiple_of(h * width, width), width)


def in_ring(value, axis, name):
    count = lax.axis_size(axis)
    with jax.named_scope(name):
        return lax.ppermute(value, axis, [(source, (source + 1) % count) for source in range(count)])


def exchanged(value, axis, offset, name):
    count = lax.axis_size(axis)
    with jax.named_scope(f"{name}{offset}"):
        return lax.ppermute(value, axis, [(source, source ^ offset) for source in range(count)])


def pool_kernel(my_ref, q_hbm, k_hbm, v_hbm, qw_hbm, kw_hbm, vw_hbm, *rest):
    heads = len(rest) - 7
    outs, (q_buf, k_buf, v_buf, qw_buf, kw_buf, vw_buf, sems) = rest[:heads], rest[heads:]
    tokens = q_hbm.shape[0]
    width = q_hbm.shape[1] // heads
    pooled = tokens // POOL_FACTOR
    my = my_ref[0]
    pairs = (
        (k_hbm, k_buf),
        (v_hbm, v_buf),
        (kw_hbm, kw_buf),
        (vw_hbm, vw_buf),
        (qw_hbm, qw_buf),
        (q_hbm, q_buf),
    )
    copies = [pltpu.make_async_copy(a, b, sems.at[i]) for i, (a, b) in enumerate(pairs)]
    for copy in copies:
        copy.start()
    row = lax.broadcasted_iota(jnp.int32, (tokens, tokens), 0)
    column = lax.broadcasted_iota(jnp.int32, (tokens, tokens), 1)
    wanted = POOL_FACTOR * (row % pooled) + row // pooled
    pick = jnp.where(column == wanted, 1.0, 0.0).astype(jnp.bfloat16)

    def weighted(rows, weights):
        picked = dot(pick, rows, NN)
        total = picked[:pooled] * weights[0:1]
        for i in range(1, POOL_FACTOR):
            total = total + picked[i * pooled : (i + 1) * pooled] * weights[i : i + 1]
        return total.astype(jnp.bfloat16)

    for copy in copies[:4]:
        copy.wait()
    for m in range(heads):
        narrow = head_columns(my ^ m)
        rows = jnp.concatenate([k_buf[:, narrow], v_buf[:, narrow]], axis=1)
        weights = jnp.concatenate([kw_buf[:, narrow], vw_buf[:, narrow]], axis=1)
        outs[m][:, width:] = weighted(rows, weights)
    for copy in copies[4:]:
        copy.wait()
    for m in range(heads):
        wide = head_columns(my ^ m, width)
        outs[m][:, :width] = weighted(q_buf[:, wide], qw_buf[:, wide])


def pool(my, queries, keys, values, qw, kw, vw):
    tokens, columns = queries.shape
    heads = keys.shape[1] // HEAD_SIZE
    width = columns // heads
    span = 2 * HEAD_SIZE
    payload = jax.ShapeDtypeStruct((tokens // POOL_FACTOR, width + span), jnp.bfloat16)
    return pl.pallas_call(
        pool_kernel,
        in_specs=[SMEM] + [ANY] * 6,
        out_specs=[VMEM] * heads,
        out_shape=[payload] * heads,
        scratch_shapes=[
            pltpu.VMEM(queries.shape, jnp.bfloat16),
            pltpu.VMEM(keys.shape, jnp.bfloat16),
            pltpu.VMEM(values.shape, jnp.bfloat16),
            pltpu.VMEM(qw.shape, jnp.float32),
            pltpu.VMEM(kw.shape, jnp.float32),
            pltpu.VMEM(vw.shape, jnp.float32),
            pltpu.SemaphoreType.DMA((6,)),
        ],
        compiler_params=params(),
        cost_estimate=cost(1000, 1000),
    )(my, *in_hbm(queries, keys, values, qw, kw, vw))


def stack_kernel(my_ref, *refs):
    payloads, out_ref = refs[:-1], refs[-1]
    sections = len(payloads)
    pooled, span = payloads[0].shape[0], out_ref.shape[1]
    width = payloads[0].shape[1] - span
    my = my_ref[0]
    parts = width // span
    row = lax.broadcasted_iota(jnp.int32, (CARRY_ROWS, span), 0)
    carry = jnp.zeros((CARRY_ROWS, span), jnp.float32)
    for m in range(sections):
        s = my ^ m
        out_ref[pl.ds(pl.multiple_of(s * pooled, pooled), pooled), :] = payloads[m][:, width:]
        last = payloads[m][pooled - 16 :, :width].astype(jnp.float32)[15:]
        for i in range(parts):
            carry = jnp.where(row == parts * s + i, last[:, i * span : (i + 1) * span], carry)
    out_ref[sections * pooled :, :] = carry.astype(jnp.bfloat16)


def stack(my, payloads):
    sections = len(payloads)
    pooled, columns = payloads[0].shape
    span = 2 * HEAD_SIZE
    return pl.pallas_call(
        stack_kernel,
        in_specs=[SMEM] + [VMEM] * sections,
        out_specs=VMEM,
        out_shape=jax.ShapeDtypeStruct((sections * pooled + CARRY_ROWS, span), jnp.bfloat16),
        compiler_params=params(),
        cost_estimate=cost(1000, 1000),
    )(my, *payloads)


def with_ones(values):
    return jnp.concatenate([values, jnp.ones_like(values)], axis=1)


def coarse_kernel(sections, seq_count, place_ref, *refs):
    payloads, blocks = refs[:sections], refs[sections : sections + seq_count]
    outs = refs[sections + seq_count : -4]
    q_buf, kv_buf, carry_buf, out_buf = refs[-4:]
    pooled = payloads[0].shape[0]
    span = kv_buf.shape[2]
    width = payloads[0].shape[1] - span
    group = width // HEAD_SIZE
    rows = group * pooled
    parts = width // span
    my, z = place_ref[0], place_ref[1]
    for m in range(sections):
        q_buf[my ^ m] = payloads[m][:, :width]
    for m in range(seq_count):
        carry_buf[z ^ m] = blocks[m][sections * pooled :, :]
        for s in range(sections):
            at = pl.ds(pl.multiple_of((z ^ m) * pooled, pooled), pooled)
            kv_buf[s, at, :] = blocks[m][s * pooled : (s + 1) * pooled, :]
    before = carry_buf[jnp.where(z == 0, seq_count - 1, z - 1)].astype(jnp.float32)
    chunk = seq_count * pooled
    row = lax.broadcasted_iota(jnp.int32, (rows, chunk), 0) % pooled
    column = lax.broadcasted_iota(jnp.int32, (rows, chunk), 1)
    allowed = column < z * pooled + row
    first = lax.broadcasted_iota(jnp.int32, (rows, HEAD_SIZE), 0) % pooled == 0
    for s in range(sections):
        q = q_buf[s].astype(jnp.float32)
        shifted = jnp.concatenate([q[-1:], q[:-1]], axis=0)
        here = before[parts * s : parts * (s + 1)]
        if s > 0:
            here = jnp.where(z == 0, before[parts * (s - 1) : parts * s], here)
        pieces = []
        for g in range(group):
            at = g * HEAD_SIZE
            piece = here[at // span : at // span + 1, at % span : at % span + HEAD_SIZE]
            pieces.append(jnp.where(first[:pooled], piece, shifted[:, at : at + HEAD_SIZE]))
        stacked = jnp.concatenate(pieces, axis=0).astype(jnp.bfloat16)
        scores = [dot(stacked, kv_buf[c, :, :HEAD_SIZE], NT) for c in range(s + 1)]
        scores[s] = jnp.where(allowed, scores[s], MASKED)
        highest = functools.reduce(jnp.maximum, scores)
        highest = jnp.max(highest, axis=1, keepdims=True)
        total = None
        for c in range(s + 1):
            weights = jnp.exp2((scores[c] - highest) * EXP2_SCALE).astype(jnp.bfloat16)
            part = dot(weights, with_ones(kv_buf[c, :, HEAD_SIZE:]), NN)
            total = part if total is None else total + part
        result = total[:, :HEAD_SIZE] / total[:, HEAD_SIZE:]
        if s == 0:
            result = jnp.where(first & (z == 0), 0.0, result)
        result = result.astype(jnp.bfloat16)
        for g in range(group):
            out_buf[s, :, g * HEAD_SIZE : (g + 1) * HEAD_SIZE] = result[g * pooled : (g + 1) * pooled]
    for m in range(sections):
        outs[m][...] = out_buf[my ^ m]


def coarse_attention(place, payloads, blocks):
    sections, seq_count = len(payloads), len(blocks)
    pooled, columns = payloads[0].shape
    span = 2 * HEAD_SIZE
    width = columns - span
    pairs = sections * pooled * width // HEAD_SIZE * sections * seq_count * pooled
    return pl.pallas_call(
        functools.partial(coarse_kernel, sections, seq_count),
        in_specs=[SMEM] + [VMEM] * (sections + seq_count),
        out_specs=[VMEM] * sections,
        out_shape=[jax.ShapeDtypeStruct((pooled, width), jnp.bfloat16)] * sections,
        scratch_shapes=[
            pltpu.VMEM((sections, pooled, width), jnp.bfloat16),
            pltpu.VMEM((sections, seq_count * pooled, span), jnp.bfloat16),
            pltpu.VMEM((seq_count, CARRY_ROWS, span), jnp.bfloat16),
            pltpu.VMEM((sections, pooled, width), jnp.bfloat16),
        ],
        compiler_params=params(),
        cost_estimate=cost(4 * pairs * HEAD_SIZE, 4 * sections * seq_count * pooled * span, pairs),
    )(place, *payloads, *blocks)


def near_kernel(pos_ref, q_hbm, k0_hbm, k1_hbm, v0_hbm, v1_hbm, acc_ref, sum_ref, max_ref, q_buf, kv_buf, sems):
    heads, tokens, width = q_buf.shape
    group = width // HEAD_SIZE
    sources = (k0_hbm, k1_hbm, v0_hbm, v1_hbm)
    whole = [pltpu.make_async_copy(ref, kv_buf.at[i], sems.at[i]) for i, ref in enumerate(sources)]

    def q_copy(h):
        return pltpu.make_async_copy(q_hbm.at[:, head_columns(h, width)], q_buf.at[h], sems.at[len(sources) + h])

    whole[0].start()
    whole[1].start()
    q_copy(0).start()
    whole[2].start()
    whole[3].start()
    for h in range(1, heads):
        q_copy(h).start()
    bias = jnp.where(pos_ref[0] >= 1, 0.0, MASKED).astype(jnp.float32)
    row = lax.broadcasted_iota(jnp.int32, (tokens, tokens), 0)
    column = lax.broadcasted_iota(jnp.int32, (tokens, tokens), 1)
    own = jnp.concatenate([column <= row] * group, axis=0)

    for copy in whole:
        copy.wait()

    def scores_of(h):
        q_copy(h).wait()
        q = jnp.concatenate([q_buf[h, :, g * HEAD_SIZE : (g + 1) * HEAD_SIZE] for g in range(group)], axis=0)
        narrow = slice(h * HEAD_SIZE, (h + 1) * HEAD_SIZE)
        return dot(q, kv_buf[0, :, narrow], NT), dot(q, kv_buf[1, :, narrow], NT)

    scores = scores_of(0)
    for h in range(heads):
        outer, inner = scores
        if h + 1 < heads:
            scores = scores_of(h + 1)
        outer = jnp.where(own, outer, MASKED)
        inner = inner + bias
        highest = jnp.max(jnp.maximum(outer, inner), axis=1, keepdims=True)
        outer = jnp.exp2((outer - highest) * EXP2_SCALE).astype(jnp.bfloat16)
        inner = jnp.exp2((inner - highest) * EXP2_SCALE).astype(jnp.bfloat16)
        narrow = slice(h * HEAD_SIZE, (h + 1) * HEAD_SIZE)
        v0, v1 = kv_buf[2, :, narrow], kv_buf[3, :, narrow]
        total = dot(outer, with_ones(v0), NN) + dot(inner, with_ones(v1), NN)
        highest = jnp.broadcast_to(highest, (group * tokens, HEAD_SIZE))
        for g in range(group):
            here = slice(g * tokens, (g + 1) * tokens)
            at = slice((h * group + g) * HEAD_SIZE, (h * group + g + 1) * HEAD_SIZE)
            acc_ref[:, at] = total[here, :HEAD_SIZE]
            sum_ref[:, at] = total[here, HEAD_SIZE:]
            max_ref[:, at] = highest[here]


def near_attention(position, queries, keys, values):
    tokens, columns = queries.shape
    heads = keys[0].shape[1] // HEAD_SIZE
    width = columns // heads
    pairs = tokens * tokens * 2 * columns // HEAD_SIZE
    return pl.pallas_call(
        near_kernel,
        in_specs=[SMEM] + [ANY] * 5,
        out_specs=[VMEM] * 3,
        out_shape=[jax.ShapeDtypeStruct((tokens, columns), jnp.float32)] * 3,
        scratch_shapes=[
            pltpu.VMEM((heads, tokens, width), jnp.bfloat16),
            pltpu.VMEM((4,) + values[0].shape, jnp.bfloat16),
            pltpu.SemaphoreType.DMA((4 + heads,)),
        ],
        compiler_params=params(),
        cost_estimate=cost(4 * pairs * HEAD_SIZE, 8 * tokens * columns, pairs),
    )(position, *in_hbm(queries, keys[0]), keys[1], *in_hbm(values[0]), values[1])


def far_kernel(pos_ref, q_hbm, k2_hbm, acc_in, sum_in, max_in, acc_ref, last_ref, q_buf, k_buf, sems):
    heads, tokens, width = q_buf.shape
    group = width // HEAD_SIZE

    k_copy = pltpu.make_async_copy(k2_hbm, k_buf, sems.at[heads])

    def q_copy(h):
        return pltpu.make_async_copy(q_hbm.at[:, head_columns(h, width)], q_buf.at[h], sems.at[h])

    k_copy.start()
    for h in range(heads):
        q_copy(h).start()
    row = lax.broadcasted_iota(jnp.int32, (tokens, tokens), 0)
    column = lax.broadcasted_iota(jnp.int32, (tokens, tokens), 1)
    seen = jnp.concatenate([(column > row) & (pos_ref[0] >= 2)] * group, axis=0)
    ones = jnp.ones((tokens, HEAD_SIZE), jnp.bfloat16)

    k_copy.wait()

    def one_head(h, carried):
        q_copy(h).wait()
        ats = [head_columns(h * group + g) for g in range(group)]
        q = jnp.concatenate([q_buf[h, :, g * HEAD_SIZE : (g + 1) * HEAD_SIZE] for g in range(group)], axis=0)
        scores = jnp.where(seen, dot(q, k_buf[:, head_columns(h)], NT), MASKED)
        before = jnp.concatenate([max_in[:, at] for at in ats], axis=0)
        highest = jnp.maximum(before, jnp.max(scores, axis=1, keepdims=True))
        spread = jnp.concatenate([highest] * (tokens // HEAD_SIZE), axis=1)
        weights = jnp.exp2((scores - spread) * EXP2_SCALE).astype(jnp.bfloat16)
        decay = jnp.exp2((before - highest) * EXP2_SCALE)
        total = jnp.concatenate([sum_in[:, at] for at in ats], axis=0) * decay + dot(weights, ones, NN)
        scale = 1.0 / total
        decay = decay * scale
        weights = (weights * jnp.concatenate([scale] * (tokens // HEAD_SIZE), axis=1)).astype(jnp.bfloat16)
        for g in range(group):
            here = slice(g * tokens, (g + 1) * tokens)
            acc_ref[:, ats[g]] = acc_in[:, ats[g]] * decay[here]
            last_ref[:, head_columns(h * group + g, tokens)] = weights[here]
        return carried

    lax.fori_loop(0, heads, one_head, 0)


def far_attention(position, queries, keys, acc, total, highest):
    tokens, columns = queries.shape
    heads = keys.shape[1] // HEAD_SIZE
    width = columns // heads
    pairs = tokens * tokens * columns // HEAD_SIZE
    return pl.pallas_call(
        far_kernel,
        in_specs=[SMEM, ANY, ANY] + [VMEM] * 3,
        out_specs=[VMEM] * 2,
        out_shape=[
            jax.ShapeDtypeStruct((tokens, columns), jnp.float32),
            jax.ShapeDtypeStruct((tokens, columns // HEAD_SIZE * tokens), jnp.bfloat16),
        ],
        scratch_shapes=[
            pltpu.VMEM((heads, tokens, width), jnp.bfloat16),
            pltpu.VMEM(keys.shape, jnp.bfloat16),
            pltpu.SemaphoreType.DMA((heads + 1,)),
        ],
        compiler_params=params(),
        cost_estimate=cost(4 * pairs * HEAD_SIZE, 12 * tokens * columns, pairs),
    )(position, *in_hbm(queries), keys, acc, total, highest)


def join_kernel(my_ref, acc_ref, last_ref, v2_hbm, up_hbm, *refs):
    sections = len(refs) - 6
    coarse, (comb_ref, sq_ref, v2_buf, up_ref, coarse_buf, sems) = refs[:sections], refs[sections:]
    copies = [
        pltpu.make_async_copy(v2_hbm, v2_buf, sems.at[0]),
        pltpu.make_async_copy(up_hbm, up_ref, sems.at[1]),
    ]
    for copy in copies:
        copy.start()
    tokens, columns = acc_ref.shape
    heads = v2_buf.shape[1] // HEAD_SIZE
    width = columns // heads
    pooled = tokens // POOL_FACTOR
    my = my_ref[0]
    for m in range(sections):
        coarse_buf[my ^ m] = coarse[m][...]
    token = lax.broadcasted_iota(jnp.int32, (tokens, pooled), 0)
    spread = jnp.where(token // POOL_FACTOR == lax.broadcasted_iota(jnp.int32, (tokens, pooled), 1), 1.0, 0.0)
    spread = spread.astype(jnp.bfloat16)
    for copy in copies:
        copy.wait()

    def one_head(h, squares):
        wide = head_columns(h, width)
        upsampled = dot(spread, coarse_buf[h], NN)
        up = up_ref[:, wide]
        up = jnp.concatenate([up, up], axis=0)
        upsampled = (upsampled.reshape(tokens // 8, 8, width) * up[None]).reshape(tokens, width)
        values = v2_buf[:, head_columns(h)]
        for g in range(width // HEAD_SIZE):
            at = h * (width // HEAD_SIZE) + g
            part = dot(last_ref[:, head_columns(at, tokens)], values, NN)
            here = slice(g * HEAD_SIZE, (g + 1) * HEAD_SIZE)
            combined = acc_ref[:, head_columns(at)] + part + upsampled[:, here]
            comb_ref[:, head_columns(at)] = combined
            squares = squares + combined * combined
        return squares

    squares = jnp.zeros((tokens, HEAD_SIZE), jnp.float32)
    for h in range(heads):
        squares = one_head(h, squares)
    sq_ref[...] = jnp.broadcast_to(jnp.sum(squares, axis=1, keepdims=True), sq_ref.shape)


def join(my, acc, last, values, up_weight, coarse):
    tokens, columns = acc.shape
    pooled, width = coarse[0].shape
    return pl.pallas_call(
        join_kernel,
        in_specs=[SMEM, VMEM, VMEM, ANY, ANY] + [VMEM] * len(coarse),
        out_specs=[VMEM, VMEM],
        out_shape=[
            jax.ShapeDtypeStruct((tokens, columns), jnp.float32),
            jax.ShapeDtypeStruct((tokens, HEAD_SIZE), jnp.float32),
        ],
        scratch_shapes=[
            pltpu.VMEM(values.shape, jnp.bfloat16),
            pltpu.VMEM(up_weight.shape, jnp.float32),
            pltpu.VMEM((len(coarse), pooled, width), jnp.bfloat16),
            pltpu.SemaphoreType.DMA((2,)),
        ],
        compiler_params=params(),
        cost_estimate=cost(2 * tokens * tokens * columns, 12 * tokens * columns),
    )(my, acc, last, values, *in_hbm(up_weight), *coarse)


def norm_kernel(full, comb_ref, mine_ref, other_ref, gain_ref, out_hbm, buf, sems):
    parts, rows, columns = buf.shape
    copies = []
    for i in range(parts):
        here = pl.ds(i * rows, rows)
        mean = (mine_ref[here, :1] + other_ref[here, :1]) / full
        buf[i] = (comb_ref[here, :] * lax.rsqrt(mean + 1e-05) * gain_ref[...]).astype(jnp.bfloat16)
        copies.append(pltpu.make_async_copy(buf.at[i], out_hbm.at[here, :], sems.at[i]))
        copies[-1].start()
    for copy in copies:
        copy.wait()


def normalized(combined, mine, other, gain, full):
    tokens, columns = combined.shape
    parts = 4
    return pl.pallas_call(
        functools.partial(norm_kernel, full),
        in_specs=[VMEM] * 4,
        out_specs=ANY,
        out_shape=jax.ShapeDtypeStruct((tokens, columns), jnp.bfloat16),
        scratch_shapes=[
            pltpu.VMEM((parts, tokens // parts, columns), jnp.bfloat16),
            pltpu.SemaphoreType.DMA((parts,)),
        ],
        compiler_params=params(),
        cost_estimate=cost(3 * tokens * columns, 6 * tokens * columns),
    )(combined, mine, other, gain)


def per_device(queries, keys, values, qw, kw, vw, up_weight, out_gain):
    tokens, columns = queries.shape
    heads = keys.shape[1] // HEAD_SIZE
    seq_count = lax.axis_size("seq")
    section_count = lax.axis_size("section")
    head_count = lax.axis_size("head")
    if WINDOW_LENGTH != 2 * tokens or heads != section_count or head_count != 2:
        raise ValueError("unsupported sizes")
    line = ("section", "seq")
    section = lax.axis_index("section")
    z = lax.axis_index("seq")
    position = section * seq_count + z
    my = section[None]
    others = range(1, section_count)

    k1 = in_ring(keys, line, "first_keys")
    payloads = list(pool(my, queries, keys, values, qw, kw, vw))
    for m in others:
        payloads[m] = exchanged(payloads[m], "section", m, "pooled_to_heads")
    *payloads, late_values = lax.optimization_barrier((*payloads, values))
    v1 = in_ring(late_values, line, "first_values")
    stacked = stack(my, payloads)
    far = exchanged(stacked, "seq", 2, "pooled_far")
    near = exchanged(stacked, "seq", 1, "pooled_near")
    acc, total, highest = near_attention(position[None], queries, (keys, k1), (values, v1))
    far, near, acc = lax.optimization_barrier((far, near, acc))
    farther = exchanged(far, "seq", 1, "pooled_farther")
    far, k1 = lax.optimization_barrier((far, k1))
    k2 = in_ring(k1, line, "second_keys")
    farther, v1 = lax.optimization_barrier((farther, v1))
    v2 = in_ring(v1, line, "second_values")
    blocks = [stacked, near, far, farther]
    coarse = list(coarse_attention(jnp.stack([section, z]), payloads, blocks))
    for m in others:
        coarse[m] = exchanged(coarse[m], "section", m, "coarse_back")
    acc, last = far_attention(position[None], queries, k2, acc, total, highest)
    combined, mine = join(my, acc, last, v2, up_weight, coarse)
    other = exchanged(mine, "head", 1, "squares")
    return normalized(combined, mine, other, out_gain[None], head_count * columns)


def solution(mesh):
    rows = P(("section", "seq"), "head")
    return jax.shard_map(
        per_device,
        mesh=mesh,
        in_specs=(rows, rows, rows, P(None, "head"), P(None, "head"), P(None, "head"), P(None, "head"), P("head")),
        out_specs=rows,
        check_vma=False,
    )
```
